32 devices in a mesh: seq: 4 (over y, x), chan: 4 (over z), rep: 2 (over core).
Axes of the slice: x: 2, y: 2, z: 4, core: 2. Of those that a mesh axis runs over, the one named last changes fastest.
Arguments:
- tokens: bfloat16 [3072, 8192], P(('rep', 'seq'), 'chan'), parts along dimension 0, may hold values from -6 to 6
- w_in: bfloat16 [1024, 3, 8192], P('chan', None, 'seq'), may hold values from -0.0625 to 0.0625
- short_taps: float32 [3, 3, 1024], P(None, None, 'chan'), may hold values from -3 to 3
- decay: float32 [16, 1024], P(None, 'chan'), may hold values from 0.00016276042 to 0.03
- residue: float32 [16, 1024], P(None, 'chan'), may hold values from -2 to 2
- skip: float32 [1024], P('chan'), may hold values from -2.5 to 2.5
- w_out: bfloat16 [1024, 8192], P(None, 'chan'), may hold values from -0.1875 to 0.1875
Outputs:
- mixed: bfloat16 [3072, 8192], P(('rep', 'seq'), 'chan'), parts along dimension 0
The draws below stay inside these ranges and needn't reach their ends.
There are 2 independent parts, one for each index of `rep`. The reference program is written for one: setup_inputs(seed, part) draws one part's arguments, and reference() takes and returns one part's arrays. A program takes and returns all parts, laid end to end along the dimension named above; an argument that names none is the same for every part. Nothing has to cross between parts.
All inputs are finite; a program needn't handle non-finite values.
Results may differ from the reference program's by a relative error of at most 0.0079.
Values may be sent and summed in bfloat16 or wider, within the bound.
A program may use at most 128 MiB of HBM per device.

```python
import math
import jax
import jax.numpy as jnp
from jax import lax

D = 8192
CH = 1024
MODES = 16
KS = 3
TOKENS = 1536


def block_levels(own_key, shape, shards, least, largest):
    factor_of = 1.0
    for axis_at, shards_of in shards:
        draws = jax.random.uniform(jax.random.fold_in(jax.random.fold_in(own_key, 6), axis_at), (shards_of,), jnp.float32, least / len(shards), largest / len(shards))
        factor_of = factor_of * jnp.repeat(jnp.exp(draws), shape[axis_at] // shards_of).reshape((-1,) + (1,) * (len(shape) - 1 - axis_at))
    return factor_of


def gaussian(stream_key, shape, deviation, reach, shards=(), kind=jnp.bfloat16):
    array = deviation * jax.random.normal(stream_key, shape, jnp.float32)
    if shards:
        array = array * block_levels(stream_key, shape, shards, -0.22, 0.18)
    return jnp.clip(array, -reach, reach).astype(kind)


def setup_inputs(seed: int = 0, part: int = 0) -> dict:
    splits = jax.random.split(jax.random.key(seed), 8)
    part_keys = jax.random.split(jax.random.fold_in(splits[7], part), 8)
    tokens = gaussian(part_keys[0], (TOKENS, D), 1.0, 6.0, ((0, 4), (1, 4)))
    w_in = gaussian(splits[1], (CH, 3, D), D ** -0.5, 0.0625, ((0, 4), (2, 4)))
    short_taps = gaussian(splits[2], (KS, 3, CH), 0.6, 3.0, ((2, 4),), jnp.float32)
    decay = jnp.clip(jnp.exp(math.log(0.03) - 5.2166733 * jax.random.uniform(splits[3], (MODES, CH), jnp.float32) ** block_levels(splits[3], (MODES, CH), ((1, 4),), -0.2, 0.2)), 0.00016276042, 0.03)
    residue = gaussian(splits[4], (MODES, CH), 0.35, 2.0, ((1, 4),), jnp.float32)
    skip = gaussian(splits[5], (CH,), 0.5, 2.5, ((0, 4),), jnp.float32)
    w_out = gaussian(splits[6], (CH, D), CH ** -0.5, 0.1875, ((1, 4),))
    return {"tokens": tokens, "w_in": w_in, "short_taps": short_taps, "decay": decay, "residue": residue, "skip": skip, "w_out": w_out}


def reference(tokens, w_in, short_taps, decay, residue, skip, w_out):
    length = tokens.shape[0]
    channels = w_in.shape[0]
    flat_w = w_in.reshape(channels * 3, w_in.shape[2])
    qkv = jnp.dot(flat_w, tokens.T, preferred_element_type=jnp.float32)
    qkv = qkv.reshape(channels, 3, length).astype(jnp.bfloat16)
    qkv_f = lax.optimization_barrier(qkv).astype(jnp.float32)
    taps_n = short_taps.shape[0]
    padded = jnp.pad(qkv_f, ((0, 0), (0, 0), (taps_n - 1, 0)))
    feat = jnp.zeros((channels, 3, length), jnp.float32)
    for j in range(taps_n):
        tap_j = short_taps[j].astype(jnp.float32).T
        feat = feat + tap_j[:, :, None] * padded[:, :, taps_n - 1 - j:taps_n - 1 - j + length]
    query = feat[:, 0]
    zprod = (feat[:, 1] * feat[:, 2]).astype(jnp.bfloat16)
    z_f = lax.optimization_barrier(zprod).astype(jnp.float32)
    times = jnp.arange(length, dtype=jnp.float32)
    filt = jnp.zeros((channels, length), jnp.float32)
    for m in range(decay.shape[0]):
        rate = decay[m][:, None]
        filt = filt + residue[m][:, None] * jnp.sqrt(rate) * jnp.exp(-rate * times[None, :])
    z_spec = jnp.fft.rfft(z_f, n=2 * length, axis=1)
    h_spec = jnp.fft.rfft(filt, n=2 * length, axis=1)
    conv = jnp.fft.irfft(z_spec * h_spec, n=2 * length, axis=1)[:, :length]
    longc = (conv + skip[:, None] * z_f).astype(jnp.bfloat16)
    long_f = lax.optimization_barrier(longc).astype(jnp.float32)
    gated = (query * long_f).astype(jnp.bfloat16)
    mixed = jnp.dot(gated.T, w_out, preferred_element_type=jnp.float32)
    return mixed.astype(jnp.bfloat16)
```

```python
import functools

import jax
import jax.numpy as jnp
from jax import lax
from jax.experimental import pallas as pl
from jax.experimental.pallas import tpu as pltpu
from jax.sharding import PartitionSpec as P

MESH = pl.DeviceIdType.MESH
F32 = jnp.float32
BF16 = jnp.bfloat16
STEP = 16
HALO = 16


def kernel(
    dims,
    tok_hbm, w_hbm, taps_ref, decay_ref, residue_ref, skip_ref, wout_hbm,
    out_ref,
    tokbuf, wbuf, woutbuf, acc, qbuf, hsend, hrecv, zbuf, query, ubuf, ssend, srecv,
    t_in, t_out, t_loc, gbuf, acc2,
    loc_sem, tsend_sem, trecv_sem, wsend_sem, wrecv_sem, xsend_sem, xrecv_sem,
    hsend_sem, hrecv_sem, ssend_sem, srecv_sem, gsend_sem, grecv_sem,
):
    n_seq, n_chan, n_rep, parts, wparts, rows, ch = dims
    modes = decay_ref.shape[0]
    half = wbuf.shape[2]
    s = lax.axis_index("seq")
    c = lax.axis_index("chan")
    r = lax.axis_index("rep")
    blocks = rows // STEP

    barrier = pltpu.get_barrier_semaphore()
    for o in range(1, n_seq):
        pl.semaphore_signal(
            barrier, inc=1, device_id={"seq": lax.rem(s + o, n_seq)}, device_id_type=MESH
        )
    for o in range(1, n_rep):
        pl.semaphore_signal(
            barrier, inc=1, device_id={"rep": lax.rem(r + o, n_rep)}, device_id_type=MESH
        )

    @pl.when(c > 0)
    def _():
        pl.semaphore_signal(barrier, inc=1, device_id={"chan": c - 1}, device_id_type=MESH)

    @pl.when(c < n_chan - 1)
    def _():
        pl.semaphore_signal(barrier, inc=1, device_id={"chan": c + 1}, device_id_type=MESH)

    own_tok = pltpu.make_async_copy(tok_hbm, tokbuf.at[c], loc_sem.at[0])
    own_w = pltpu.make_async_copy(
        w_hbm, wbuf.at[:, pl.ds(s * wparts, wparts)], loc_sem.at[1]
    )
    own_wout = pltpu.make_async_copy(wout_hbm, woutbuf, loc_sem.at[2])
    own_tok.start()
    own_w.start()
    own_wout.start()

    peers = n_seq - 1 + n_rep - 1
    at_end = (c == 0) | (c == n_chan - 1)

    @pl.when(at_end)
    def _():
        pl.semaphore_wait(barrier, peers + min(1, n_chan - 1))

    @pl.when(jnp.logical_not(at_end))
    def _():
        pl.semaphore_wait(barrier, peers + 2)

    def tok_copy(block, k, way, own):
        src = tok_hbm.at[k] if own else tokbuf.at[block, k]
        return pltpu.make_async_remote_copy(
            src_ref=src,
            dst_ref=tokbuf.at[block, k],
            send_sem=tsend_sem.at[way, block, k],
            recv_sem=trecv_sem.at[block, k],
            device_id={"chan": c + (1 if way == 0 else -1)},
            device_id_type=MESH,
        )

    def can_send(way):
        return c < n_chan - 1 if way == 0 else c > 0

    def source(way, d):
        block = c - d if way == 0 else c + d
        there = block >= 0 if way == 0 else block <= n_chan - 1
        return block, there

    for k in range(parts):
        for way in range(2):
            @pl.when(can_send(way))
            def _():
                tok_copy(c, k, way, True).start()

    def w_copy(o, incoming):
        to = lax.rem(s + o, n_seq)
        block = lax.rem(s + n_seq - o, n_seq) if incoming else s
        return pltpu.make_async_remote_copy(
            src_ref=w_hbm.at[r],
            dst_ref=wbuf.at[r, pl.ds(block * wparts, wparts)],
            send_sem=wsend_sem.at[o],
            recv_sem=wrecv_sem.at[o],
            device_id={"seq": to},
            device_id_type=MESH,
        )

    for o in range(1, n_seq):
        w_copy(o, False).start()

    def x_copy(o, p, incoming):
        block = lax.rem(s + n_seq - o, n_seq)
        which = lax.rem(r + n_rep - p, n_rep) if incoming else r
        place = wbuf.at[which, pl.ds(block * wparts, wparts)]
        return pltpu.make_async_remote_copy(
            src_ref=place,
            dst_ref=place,
            send_sem=xsend_sem.at[o, p],
            recv_sem=xrecv_sem.at[o, p],
            device_id={"rep": lax.rem(r + p, n_rep)},
            device_id_type=MESH,
        )

    rate = decay_ref[...]
    amp = residue_ref[...] * jnp.sqrt(rate)
    step_of = lax.broadcasted_iota(jnp.int32, (STEP, ch), 0)
    for m in range(modes):
        t_out[m] = amp[m : m + 1] * jnp.exp(-rate[m : m + 1] * step_of.astype(F32))
    filt = t_out[0]
    for m in range(1, modes):
        filt = filt + t_out[m]
    for i in range(STEP):
        t_in[i] = jnp.exp(-rate * float(STEP - i))
        if i == 0:
            t_loc[i] = filt
        else:
            t_loc[i] = jnp.concatenate([jnp.zeros((i, ch), F32), filt[: STEP - i]], axis=0)
    acc[...] = jnp.zeros_like(acc)

    def arrive(d, then):
        for k in range(parts):
            for way in range(2):
                block, there = source(way, d)

                @pl.when(there)
                def _():
                    tok_copy(block, k, way, False).wait_recv()

                    if d < n_chan - 1:
                        @pl.when(can_send(way))
                        def _():
                            tok_copy(block, k, way, False).start()

                    if then:
                        multiply(block, k)

    def multiply(block, k):
        j = block * parts + k
        a = tokbuf[block, k]
        for h in range(n_rep):
            acc[:, h * half : (h + 1) * half] += lax.dot_general(
                a, wbuf[h, j], (((1,), (1,)), ((), ())), preferred_element_type=F32
            )

    for d in range(1, n_chan - 1):
        arrive(d, False)
    for o in range(1, n_seq):
        w_copy(o, True).wait_recv()
        for p in range(1, n_rep):
            x_copy(o, p, False).start()
    own_tok.wait()
    own_w.wait()
    for o in range(1, n_seq):
        for p in range(1, n_rep):
            x_copy(o, p, True).wait_recv()

    def early(i, carry):
        block = i // parts
        k = lax.rem(i, parts)
        off = block - c

        @pl.when((off < n_chan - 1) & (off > 1 - n_chan))
        def _():
            multiply(block, k)

        return carry

    lax.fori_loop(0, n_chan * parts, early, 0)
    if n_chan > 1:
        arrive(n_chan - 1, True)

    qbuf[HALO:, :] = acc[...].astype(BF16).astype(F32)
    hsend[...] = qbuf[rows:, :].astype(BF16)
    halo_copy = pltpu.make_async_remote_copy(
        src_ref=hsend,
        dst_ref=hrecv,
        send_sem=hsend_sem,
        recv_sem=hrecv_sem,
        device_id={"seq": lax.rem(s + 1, n_seq)},
        device_id_type=MESH,
    )

    @pl.when(s < n_seq - 1)
    def _():
        halo_copy.start()

    @pl.when(s > 0)
    def _():
        halo_copy.wait_recv()
        qbuf[:HALO, :] = hrecv[...].astype(F32)

    @pl.when(s == 0)
    def _():
        qbuf[:HALO, :] = jnp.zeros((HALO, 3 * ch), F32)

    leap = jnp.exp(-rate * float(STEP))

    def first(b, state):
        base = pl.multiple_of(b * STEP, STEP)
        feats = []
        for g in range(3):
            window = qbuf[pl.ds(base + 8, STEP + 8), g * ch : (g + 1) * ch]
            feat = taps_ref[g : g + 1] * window[8:]
            for j in range(1, 3):
                row = j * 3 + g
                feat = feat + taps_ref[row : row + 1] * window[8 - j : 8 - j + STEP]
            feats.append(feat)
        z = (feats[1] * feats[2]).astype(BF16).astype(F32)
        query[pl.ds(base, STEP), :] = feats[0]
        zbuf[pl.ds(base, STEP), :] = z
        grown = t_in[0] * z[0:1]
        for i in range(1, STEP):
            grown = grown + t_in[i] * z[i : i + 1]
        ubuf[b] = grown
        return leap * state + grown

    ssend[...] = lax.fori_loop(0, blocks, first, jnp.zeros((modes, ch), F32))

    def s_copy(o):
        return pltpu.make_async_remote_copy(
            src_ref=ssend,
            dst_ref=srecv.at[o],
            send_sem=ssend_sem.at[o],
            recv_sem=srecv_sem.at[o],
            device_id={"seq": lax.rem(s + o, n_seq)},
            device_id_type=MESH,
        )

    for o in range(1, n_seq):
        @pl.when(s + o < n_seq)
        def _():
            s_copy(o).start()

    acc2[:modes, :ch] = jnp.zeros((modes, ch), F32)
    for o in range(1, n_seq):
        @pl.when(s >= o)
        def _():
            s_copy(o).wait_recv()
            acc2[:modes, :ch] += jnp.exp(-rate * float(rows * (o - 1))) * srecv[o]

    skip = skip_ref[...]

    def second(b, state):
        base = pl.multiple_of(b * STEP, STEP)
        z = zbuf[pl.ds(base, STEP), :]
        total = skip * z
        for i in range(STEP):
            total = total + t_loc[i] * z[i : i + 1]
        for m in range(modes):
            total = total + t_out[m] * state[m : m + 1]
        longc = total.astype(BF16).astype(F32)
        gbuf[c, pl.ds(base, STEP), :] = (query[pl.ds(base, STEP), :] * longc).astype(BF16)
        return leap * state + ubuf[b]

    lax.fori_loop(0, blocks, second, acc2[:modes, :ch])

    def g_copy(block, way):
        return pltpu.make_async_remote_copy(
            src_ref=gbuf.at[block],
            dst_ref=gbuf.at[block],
            send_sem=gsend_sem.at[way, block],
            recv_sem=grecv_sem.at[block],
            device_id={"chan": c + (1 if way == 0 else -1)},
            device_id_type=MESH,
        )

    for way in range(2):
        @pl.when(can_send(way))
        def _():
            g_copy(c, way).start()

    own_wout.wait()
    width = acc2.shape[1]
    tile = min(512, width)

    def project(block, opening):
        def one(i, carry):
            cols = pl.ds(pl.multiple_of(i * tile, tile), tile)
            part = jnp.dot(gbuf[block], woutbuf[block, :, cols], preferred_element_type=F32)
            if opening:
                acc2[:, cols] = part
            else:
                acc2[:, cols] += part
            return carry

        lax.fori_loop(0, width // tile, one, 0)

    project(c, True)
    for d in range(1, n_chan):
        for way in range(2):
            block, there = source(way, d)

            @pl.when(there)
            def _():
                g_copy(block, way).wait_recv()

                if d < n_chan - 1:
                    @pl.when(can_send(way))
                    def _():
                        g_copy(block, way).start()

                project(block, False)
    out_ref[...] = acc2[...].astype(BF16)

    for d in range(n_chan - 1):
        for way in range(2):
            block, there = source(way, d)

            @pl.when(there & can_send(way))
            def _():
                for k in range(parts):
                    tok_copy(block, k, way, d == 0).wait_send()
                g_copy(block, way).wait_send()

    for o in range(1, n_seq):
        w_copy(o, False).wait_send()
        for p in range(1, n_rep):
            x_copy(o, p, False).wait_send()

        @pl.when(s + o < n_seq)
        def _():
            s_copy(o).wait_send()

    @pl.when(s < n_seq - 1)
    def _():
        halo_copy.wait_send()


def on_device(tokens, w_in, short_taps, decay, residue, skip, w_out):
    n_seq, n_chan, n_rep = (lax.axis_size(a) for a in ("seq", "chan", "rep"))
    rows, depth = tokens.shape
    ch, branches, wdepth = w_in.shape
    modes = decay.shape[0]
    width = w_out.shape[1]
    piece = min(depth // 4, wdepth)
    parts, wparts = depth // piece, wdepth // piece
    half = branches * ch // n_rep
    tok = tokens.reshape(rows, parts, piece).transpose(1, 0, 2)
    w = w_in.reshape(ch, branches, wparts, piece).transpose(2, 1, 0, 3)
    w = w.reshape(wparts, n_rep, half, piece).transpose(1, 0, 2, 3)
    taps = short_taps.reshape(short_taps.shape[0] * branches, ch)
    dims = (n_seq, n_chan, n_rep, parts, wparts, rows, ch)
    vmem = pl.BlockSpec(memory_space=pltpu.VMEM)
    hbm = pl.BlockSpec(memory_space=pl.ANY)
    dma = pltpu.SemaphoreType.DMA
    return pl.pallas_call(
        functools.partial(kernel, dims),
        out_shape=jax.ShapeDtypeStruct((rows, width), BF16),
        in_specs=[hbm, hbm, vmem, vmem, vmem, vmem, hbm],
        out_specs=vmem,
        scratch_shapes=[
            pltpu.VMEM((n_chan, parts, rows, piece), BF16),
            pltpu.VMEM((n_rep, n_seq * wparts, half, piece), BF16),
            pltpu.VMEM((n_chan, ch, width), BF16),
            pltpu.VMEM((rows, branches * ch), F32),
            pltpu.VMEM((rows + HALO, branches * ch), F32),
            pltpu.VMEM((HALO, branches * ch), BF16),
            pltpu.VMEM((HALO, branches * ch), BF16),
            pltpu.VMEM((rows, ch), F32),
            pltpu.VMEM((rows, ch), F32),
            pltpu.VMEM((rows // STEP, modes, ch), F32),
            pltpu.VMEM((modes, ch), F32),
            pltpu.VMEM((n_seq, modes, ch), F32),
            pltpu.VMEM((STEP, modes, ch), F32),
            pltpu.VMEM((modes, STEP, ch), F32),
            pltpu.VMEM((STEP, STEP, ch), F32),
            pltpu.VMEM((n_chan, rows, ch), BF16),
            pltpu.VMEM((rows, width), F32),
            dma((3,)),
            dma((2, n_chan, parts)),
            dma((n_chan, parts)),
            dma((n_seq,)),
            dma((n_seq,)),
            dma((n_seq, n_rep)),
            dma((n_seq, n_rep)),
            dma(()),
            dma(()),
            dma((n_seq,)),
            dma((n_seq,)),
            dma((2, n_chan)),
            dma((n_chan,)),
        ],
        compiler_params=pltpu.CompilerParams(
            collective_id=0, has_side_effects=True, vmem_limit_bytes=56 * 1024 * 1024
        ),
        cost_estimate=pl.CostEstimate(
            flops=2 * rows * (n_chan * depth * branches * ch + n_chan * ch * width),
            bytes_accessed=2 * (rows * depth + branches * ch * wdepth + n_chan * ch * width),
            transcendentals=0,
        ),
    )(tok, w, taps, decay, residue, skip.reshape(1, ch), w_out.reshape(n_chan, ch, width))


def solution(mesh):
    placed = (
        P(("rep", "seq"), "chan"),
        P("chan", None, "seq"),
        P(None, None, "chan"),
        P(None, "chan"),
        P(None, "chan"),
        P("chan"),
        P(None, "chan"),
    )
    return jax.shard_map(
        on_device, mesh=mesh, in_specs=placed, out_specs=P(("rep", "seq"), "chan"), check_vma=False
    )
```

```python
import functools

import jax
import jax.numpy as jnp
from jax import lax
from jax.experimental import pallas as pl
from jax.experimental.pallas import tpu as pltpu
from jax.sharding import PartitionSpec as P

MESH = pl.DeviceIdType.MESH
F32 = jnp.float32
BF16 = jnp.bfloat16
STEP = 16
HALO = 16


def kernel(
    dims,
    tok_hbm, w_hbm, taps_ref, decay_ref, residue_ref, skip_ref, wout_hbm,
    out_ref,
    tokbuf, wbuf, woutbuf, acc, qbuf, hsend, hrecv, local, query, ubuf, ssend, srecv,
    t_in, t_out, t_loc, gbuf, acc2,
    loc_sem, tsend_sem, trecv_sem, wsend_sem, wrecv_sem, xsend_sem, xrecv_sem,
    hsend_sem, hrecv_sem, ssend_sem, srecv_sem, gsend_sem, grecv_sem,
):
    n_seq, n_chan, n_rep, parts, piece, rows, ch = dims
    modes = decay_ref.shape[0]
    half, wdepth = wbuf.shape[2:]
    depth = tokbuf.shape[2]
    group = rows // parts
    order = [parts - 1] + list(range(parts - 1))
    s = lax.axis_index("seq")
    c = lax.axis_index("chan")
    r = lax.axis_index("rep")
    blocks = rows // STEP

    barrier = pltpu.get_barrier_semaphore()
    for o in range(1, n_seq):
        pl.semaphore_signal(
            barrier, inc=1, device_id={"seq": lax.rem(s + o, n_seq)}, device_id_type=MESH
        )
    for o in range(1, n_rep):
        pl.semaphore_signal(
            barrier, inc=1, device_id={"rep": lax.rem(r + o, n_rep)}, device_id_type=MESH
        )

    @pl.when(c > 0)
    def _():
        pl.semaphore_signal(barrier, inc=1, device_id={"chan": c - 1}, device_id_type=MESH)

    @pl.when(c < n_chan - 1)
    def _():
        pl.semaphore_signal(barrier, inc=1, device_id={"chan": c + 1}, device_id_type=MESH)

    own_tok = pltpu.make_async_copy(tok_hbm, tokbuf.at[c], loc_sem.at[0])
    own_w = [
        pltpu.make_async_copy(w_hbm.at[h], wbuf.at[h, s], loc_sem.at[2 + h]) for h in range(n_rep)
    ]
    own_wout = pltpu.make_async_copy(wout_hbm, woutbuf, loc_sem.at[1])
    own_tok.start()
    for copy in own_w:
        copy.start()
    own_wout.start()

    peers = n_seq - 1 + n_rep - 1
    at_end = (c == 0) | (c == n_chan - 1)

    @pl.when(at_end)
    def _():
        pl.semaphore_wait(barrier, peers + min(1, n_chan - 1))

    @pl.when(jnp.logical_not(at_end))
    def _():
        pl.semaphore_wait(barrier, peers + 2)

    def tok_copy(block, k, way, own):
        span = pl.ds(k * group, group)
        return pltpu.make_async_remote_copy(
            src_ref=tok_hbm.at[span] if own else tokbuf.at[block, span],
            dst_ref=tokbuf.at[block, span],
            send_sem=tsend_sem.at[way, block, k],
            recv_sem=trecv_sem.at[block, k],
            device_id={"chan": c + (1 if way == 0 else -1)},
            device_id_type=MESH,
        )

    def can_send(way):
        return c < n_chan - 1 if way == 0 else c > 0

    def source(way, d):
        block = c - d if way == 0 else c + d
        there = block >= 0 if way == 0 else block <= n_chan - 1
        return block, there

    for k in order:
        for way in range(2):
            @pl.when(can_send(way))
            def _():
                tok_copy(c, k, way, True).start()

    def w_copy(o, incoming):
        to = lax.rem(s + o, n_seq)
        block = lax.rem(s + n_seq - o, n_seq) if incoming else s
        return pltpu.make_async_remote_copy(
            src_ref=w_hbm.at[r],
            dst_ref=wbuf.at[r, block],
            send_sem=wsend_sem.at[o],
            recv_sem=wrecv_sem.at[o],
            device_id={"seq": to},
            device_id_type=MESH,
        )

    for o in range(1, n_seq):
        w_copy(o, False).start()

    def x_copy(o, p, incoming):
        block = lax.rem(s + n_seq - o, n_seq)
        which = lax.rem(r + n_rep - p, n_rep) if incoming else r
        place = wbuf.at[which, block]
        return pltpu.make_async_remote_copy(
            src_ref=place,
            dst_ref=place,
            send_sem=xsend_sem.at[o, p],
            recv_sem=xrecv_sem.at[o, p],
            device_id={"rep": lax.rem(r + p, n_rep)},
            device_id_type=MESH,
        )

    rate = decay_ref[...]
    amp = residue_ref[...] * jnp.sqrt(rate)
    step_of = lax.broadcasted_iota(jnp.int32, (STEP, ch), 0)
    for m in range(modes):
        t_out[m] = amp[m : m + 1] * jnp.exp(-rate[m : m + 1] * step_of.astype(F32))
    filt = t_out[0]
    for m in range(1, modes):
        filt = filt + t_out[m]
    for i in range(STEP):
        t_in[i] = jnp.exp(-rate * float(STEP - i))
        if i == 0:
            t_loc[i] = filt
        else:
            t_loc[i] = jnp.concatenate([jnp.zeros((i, ch), F32), filt[: STEP - i]], axis=0)
    acc[...] = jnp.zeros_like(acc)

    def multiply(block, span, h):
        def one(i, carry):
            off = pl.multiple_of(i * piece, piece)
            at = block * depth + off
            cols = pl.ds(pl.multiple_of(lax.rem(at, wdepth), piece), piece)
            outs = pl.ds(pl.multiple_of(h * half, 128), half)
            acc[span, outs] += lax.dot_general(
                tokbuf[block, span, pl.ds(off, piece)],
                wbuf[h, at // wdepth, :, cols],
                (((1,), (1,)), ((), ())),
                preferred_element_type=F32,
            )
            return carry

        lax.fori_loop(0, depth // piece, one, 0)

    for d in range(1, n_chan - 1):
        for k in order:
            for way in range(2):
                block, there = source(way, d)

                @pl.when(there)
                def _():
                    tok_copy(block, k, way, False).wait_recv()

                    @pl.when(can_send(way))
                    def _():
                        tok_copy(block, k, way, False).start()

    for o in range(1, n_seq):
        w_copy(o, True).wait_recv()
        for p in range(1, n_rep):
            x_copy(o, p, False).start()
    own_tok.wait()
    for copy in own_w:
        copy.wait()

    def early(h):
        def one(block, carry):
            off = block - c

            @pl.when((off < max(1, n_chan - 1)) & (off > -max(1, n_chan - 1)))
            def _():
                multiply(block, pl.ds(0, rows), h)

            return carry

        lax.fori_loop(0, n_chan, one, 0)

    early(r)
    for p in range(1, n_rep):
        for o in range(1, n_seq):
            x_copy(o, p, True).wait_recv()
        early(lax.rem(r + n_rep - p, n_rep))

    halo_copy = pltpu.make_async_remote_copy(
        src_ref=hsend,
        dst_ref=hrecv,
        send_sem=hsend_sem,
        recv_sem=hrecv_sem,
        device_id={"seq": lax.rem(s + 1, n_seq)},
        device_id_type=MESH,
    )
    skip = skip_ref[...]

    def first(b, carry):
        base = pl.multiple_of(b * STEP, STEP)
        feats = []
        for g in range(3):
            window = qbuf[pl.ds(base + 8, STEP + 8), g * ch : (g + 1) * ch]
            feat = taps_ref[g : g + 1] * window[8:]
            for j in range(1, 3):
                row = j * 3 + g
                feat = feat + taps_ref[row : row + 1] * window[8 - j : 8 - j + STEP]
            feats.append(feat)
        z = (feats[1] * feats[2]).astype(BF16).astype(F32)
        query[pl.ds(base, STEP), :] = feats[0]
        grown = t_in[0] * z[0:1]
        total = skip * z + t_loc[0] * z[0:1]
        for i in range(1, STEP):
            grown = grown + t_in[i] * z[i : i + 1]
            total = total + t_loc[i] * z[i : i + 1]
        ubuf[b] = grown
        local[pl.ds(base, STEP), :] = total
        return carry

    per = group // STEP
    for k in order:
        span = pl.ds(k * group, group)
        if n_chan > 1:
            for way in range(2):
                block, there = source(way, n_chan - 1)

                @pl.when(there)
                def _():
                    tok_copy(block, k, way, False).wait_recv()
                    for h in range(n_rep):
                        multiply(block, span, h)

        qbuf[HALO + k * group : HALO + (k + 1) * group, :] = acc[span, :].astype(BF16).astype(F32)
        if k == parts - 1:
            hsend[...] = qbuf[rows:, :].astype(BF16)

            @pl.when(s < n_seq - 1)
            def _():
                halo_copy.start()

            lax.fori_loop(k * per + 1, blocks, first, 0)
        else:
            if k == 0:
                @pl.when(s > 0)
                def _():
                    halo_copy.wait_recv()
                    qbuf[:HALO, :] = hrecv[...].astype(F32)

                @pl.when(s == 0)
                def _():
                    qbuf[:HALO, :] = jnp.zeros((HALO, 3 * ch), F32)

            lax.fori_loop(k * per, (k + 1) * per + (1 if k == parts - 2 else 0), first, 0)

    leap = jnp.exp(-rate * float(STEP))

    def scan(b, state):
        return leap * state + ubuf[b]

    ssend[...] = lax.fori_loop(0, blocks, scan, jnp.zeros((modes, ch), F32))

    def s_copy(o):
        return pltpu.make_async_remote_copy(
            src_ref=ssend,
            dst_ref=srecv.at[o],
            send_sem=ssend_sem.at[o],
            recv_sem=srecv_sem.at[o],
            device_id={"seq": lax.rem(s + o, n_seq)},
            device_id_type=MESH,
        )

    for o in range(1, n_seq):
        @pl.when(s + o < n_seq)
        def _():
            s_copy(o).start()

    acc2[:modes, :ch] = jnp.zeros((modes, ch), F32)
    for o in range(1, n_seq):
        @pl.when(s >= o)
        def _():
            s_copy(o).wait_recv()
            acc2[:modes, :ch] += jnp.exp(-rate * float(rows * (o - 1))) * srecv[o]

    def second(b, state):
        base = pl.multiple_of(b * STEP, STEP)
        total = local[pl.ds(base, STEP), :]
        for m in range(modes):
            total = total + t_out[m] * state[m : m + 1]
        longc = total.astype(BF16).astype(F32)
        gbuf[c, pl.ds(base, STEP), :] = (query[pl.ds(base, STEP), :] * longc).astype(BF16)
        return leap * state + ubuf[b]

    def g_copy(block, k, way):
        place = gbuf.at[block, pl.ds(k * group, group)]
        return pltpu.make_async_remote_copy(
            src_ref=place,
            dst_ref=place,
            send_sem=gsend_sem.at[way, block, k],
            recv_sem=grecv_sem.at[block, k],
            device_id={"chan": c + (1 if way == 0 else -1)},
            device_id_type=MESH,
        )

    state = acc2[:modes, :ch]
    for k in range(parts):
        state = lax.fori_loop(k * per, (k + 1) * per, second, state)
        for way in range(2):
            @pl.when(can_send(way))
            def _():
                g_copy(c, k, way).start()

    own_wout.wait()
    width = acc2.shape[1]
    tile = min(512, width)

    def project(block, opening):
        def one(i, carry):
            cols = pl.ds(pl.multiple_of(i * tile, tile), tile)
            part = jnp.dot(gbuf[block], woutbuf[block, :, cols], preferred_element_type=F32)
            if opening:
                acc2[:, cols] = part
            else:
                acc2[:, cols] += part
            return carry

        lax.fori_loop(0, width // tile, one, 0)

    project(c, True)
    for d in range(1, n_chan):
        for k in range(parts):
            for way in range(2):
                block, there = source(way, d)

                @pl.when(there)
                def _():
                    g_copy(block, k, way).wait_recv()

                    if d < n_chan - 1:
                        @pl.when(can_send(way))
                        def _():
                            g_copy(block, k, way).start()

        for e in range(1, n_chan - 1) if d == n_chan - 2 else [d] if d == n_chan - 1 else []:
            for way in range(2):
                block, there = source(way, e)

                @pl.when(there)
                def _():
                    project(block, False)

    out_ref[...] = acc2[...].astype(BF16)

    for d in range(n_chan - 1):
        for way in range(2):
            block, there = source(way, d)

            @pl.when(there & can_send(way))
            def _():
                for k in range(parts):
                    tok_copy(block, k, way, d == 0).wait_send()
                    g_copy(block, k, way).wait_send()

    for o in range(1, n_seq):
        w_copy(o, False).wait_send()
        for p in range(1, n_rep):
            x_copy(o, p, False).wait_send()

        @pl.when(s + o < n_seq)
        def _():
            s_copy(o).wait_send()

    @pl.when(s < n_seq - 1)
    def _():
        halo_copy.wait_send()


def on_device(tokens, w_in, short_taps, decay, residue, skip, w_out):
    n_seq, n_chan, n_rep = (lax.axis_size(a) for a in ("seq", "chan", "rep"))
    rows, depth = tokens.shape
    ch, branches, wdepth = w_in.shape
    modes = decay.shape[0]
    width = w_out.shape[1]
    piece = min(512, depth, wdepth)
    parts = 4
    half = branches * ch // n_rep
    w = w_in.transpose(1, 0, 2).reshape(n_rep, half, wdepth)
    taps = short_taps.reshape(short_taps.shape[0] * branches, ch)
    dims = (n_seq, n_chan, n_rep, parts, piece, rows, ch)
    vmem = pl.BlockSpec(memory_space=pltpu.VMEM)
    hbm = pl.BlockSpec(memory_space=pl.ANY)
    dma = pltpu.SemaphoreType.DMA
    return pl.pallas_call(
        functools.partial(kernel, dims),
        out_shape=jax.ShapeDtypeStruct((rows, width), BF16),
        in_specs=[hbm, hbm, vmem, vmem, vmem, vmem, hbm],
        out_specs=vmem,
        scratch_shapes=[
            pltpu.VMEM((n_chan, rows, depth), BF16),
            pltpu.VMEM((n_rep, n_seq, half, wdepth), BF16),
            pltpu.VMEM((n_chan, ch, width), BF16),
            pltpu.VMEM((rows, branches * ch), F32),
            pltpu.VMEM((rows + HALO, branches * ch), F32),
            pltpu.VMEM((HALO, branches * ch), BF16),
            pltpu.VMEM((HALO, branches * ch), BF16),
            pltpu.VMEM((rows, ch), F32),
            pltpu.VMEM((rows, ch), F32),
            pltpu.VMEM((rows // STEP, modes, ch), F32),
            pltpu.VMEM((modes, ch), F32),
            pltpu.VMEM((n_seq, modes, ch), F32),
            pltpu.VMEM((STEP, modes, ch), F32),
            pltpu.VMEM((modes, STEP, ch), F32),
            pltpu.VMEM((STEP, STEP, ch), F32),
            pltpu.VMEM((n_chan, rows, ch), BF16),
            pltpu.VMEM((rows, width), F32),
            dma((2 + n_rep,)),
            dma((2, n_chan, parts)),
            dma((n_chan, parts)),
            dma((n_seq,)),
            dma((n_seq,)),
            dma((n_seq, n_rep)),
            dma((n_seq, n_rep)),
            dma(()),
            dma(()),
            dma((n_seq,)),
            dma((n_seq,)),
            dma((2, n_chan, parts)),
            dma((n_chan, parts)),
        ],
        compiler_params=pltpu.CompilerParams(
            collective_id=0, has_side_effects=True, vmem_limit_bytes=56 * 1024 * 1024
        ),
        cost_estimate=pl.CostEstimate(
            flops=2 * rows * (n_chan * depth * branches * ch + n_chan * ch * width),
            bytes_accessed=2 * (rows * depth + branches * ch * wdepth + n_chan * ch * width),
            transcendentals=0,
        ),
    )(tokens, w, taps, decay, residue, skip.reshape(1, ch), w_out.reshape(n_chan, ch, width))


def solution(mesh):
    placed = (
        P(("rep", "seq"), "chan"),
        P("chan", None, "seq"),
        P(None, None, "chan"),
        P(None, "chan"),
        P(None, "chan"),
        P("chan"),
        P(None, "chan"),
    )
    return jax.shard_map(
        on_device, mesh=mesh, in_specs=placed, out_specs=P(("rep", "seq"), "chan"), check_vma=False
    )
```

```python
import functools

import jax
import jax.numpy as jnp
from jax import lax
from jax.experimental import pallas as pl
from jax.experimental.pallas import tpu as pltpu
from jax.sharding import PartitionSpec as P

MESH = pl.DeviceIdType.MESH
F32 = jnp.float32
BF16 = jnp.bfloat16
STEP = 16
HALO = 16


def kernel(
    dims,
    tok_hbm, w_hbm, taps_ref, decay_ref, residue_ref, skip_ref, wout_hbm,
    out_ref,
    tokbuf, wbuf, woutbuf, acc, qbuf, hsend, hrecv, local, query, ubuf, ssend, srecv,
    t_in, t_out, t_loc, gbuf, acc2, pbuf, pacc, psend, precv,
    loc_sem, tsend_sem, trecv_sem, wsend_sem, wrecv_sem, xsend_sem, xrecv_sem,
    fsend_sem, frecv_sem, ysend_sem, yrecv_sem, psend_sem, precv_sem,
    hsend_sem, hrecv_sem, ssend_sem, srecv_sem, gsend_sem, grecv_sem,
):
    n_seq, n_chan, n_rep, parts, piece, rows, ch = dims
    modes = decay_ref.shape[0]
    half, wdepth = wbuf.shape[2:]
    depth = tokbuf.shape[2]
    group = rows // parts
    proxied = n_chan == 4 and n_seq == n_chan and depth == wdepth
    wparts = 4 if proxied else 1
    wpiece = wdepth // wparts
    order = [parts - 1] + list(range(parts - 1))
    s = lax.axis_index("seq")
    c = lax.axis_index("chan")
    r = lax.axis_index("rep")
    blocks = rows // STEP

    barrier = pltpu.get_barrier_semaphore()
    for o in range(1, n_seq):
        pl.semaphore_signal(
            barrier, inc=1, device_id={"seq": lax.rem(s + o, n_seq)}, device_id_type=MESH
        )
    for o in range(1, n_rep):
        pl.semaphore_signal(
            barrier, inc=1, device_id={"rep": lax.rem(r + o, n_rep)}, device_id_type=MESH
        )

    @pl.when(c > 0)
    def _():
        pl.semaphore_signal(barrier, inc=1, device_id={"chan": c - 1}, device_id_type=MESH)

    @pl.when(c < n_chan - 1)
    def _():
        pl.semaphore_signal(barrier, inc=1, device_id={"chan": c + 1}, device_id_type=MESH)

    own_tok = pltpu.make_async_copy(tok_hbm, tokbuf.at[c], loc_sem.at[0])
    own_w = [
        pltpu.make_async_copy(w_hbm.at[h], wbuf.at[h, s], loc_sem.at[2 + h]) for h in range(n_rep)
    ]
    own_wout = pltpu.make_async_copy(wout_hbm, woutbuf, loc_sem.at[1])
    own_tok.start()
    for copy in own_w:
        copy.start()
    own_wout.start()

    peers = n_seq - 1 + n_rep - 1
    at_end = (c == 0) | (c == n_chan - 1)

    @pl.when(at_end)
    def _():
        pl.semaphore_wait(barrier, peers + min(1, n_chan - 1))

    @pl.when(jnp.logical_not(at_end))
    def _():
        pl.semaphore_wait(barrier, peers + 2)

    def tok_copy(block, k, way, own):
        span = pl.ds(k * group, group)
        return pltpu.make_async_remote_copy(
            src_ref=tok_hbm.at[span] if own else tokbuf.at[block, span],
            dst_ref=tokbuf.at[block, span],
            send_sem=tsend_sem.at[way, block, k],
            recv_sem=trecv_sem.at[block, k],
            device_id={"chan": c + (1 if way == 0 else -1)},
            device_id_type=MESH,
        )

    def can_send(way):
        return c < n_chan - 1 if way == 0 else c > 0

    def source(way, d):
        block = c - d if way == 0 else c + d
        there = block >= 0 if way == 0 else block <= n_chan - 1
        return block, there

    for k in order:
        for way in range(2):
            @pl.when(can_send(way))
            def _():
                tok_copy(c, k, way, True).start()

    def w_copy(o, q, incoming):
        cols = pl.ds(q * wpiece, wpiece)
        to = lax.rem(s + o, n_seq)
        block = lax.rem(s + n_seq - o, n_seq) if incoming else s
        return pltpu.make_async_remote_copy(
            src_ref=w_hbm.at[r, :, cols],
            dst_ref=wbuf.at[r, block, :, cols],
            send_sem=wsend_sem.at[o, q],
            recv_sem=wrecv_sem.at[o, q],
            device_id={"seq": to},
            device_id_type=MESH,
        )

    for q in range(wparts):
        for o in range(1, n_seq):
            w_copy(o, q, False).start()

    at_low = c == 0
    far = jnp.where(c < n_chan // 2, n_chan - 1, 0)
    far_o = lax.rem(s + n_seq - far, n_seq)
    inner = jnp.where(at_low, c + 1, c - 1)
    outer = jnp.where(c == 1, c - 1, c + 1)

    def f_copy(q):
        cols = pl.ds(q * wpiece, wpiece)
        return pltpu.make_async_remote_copy(
            src_ref=wbuf.at[r, far, :, cols],
            dst_ref=pbuf.at[r, :, cols],
            send_sem=fsend_sem.at[q],
            recv_sem=frecv_sem.at[q],
            device_id={"chan": inner},
            device_id_type=MESH,
        )

    def y_copy(p, q, incoming):
        which = lax.rem(r + n_rep - p, n_rep) if incoming else r
        place = pbuf.at[which, :, pl.ds(q * wpiece, wpiece)]
        return pltpu.make_async_remote_copy(
            src_ref=place,
            dst_ref=place,
            send_sem=ysend_sem.at[p, q],
            recv_sem=yrecv_sem.at[p, q],
            device_id={"rep": lax.rem(r + p, n_rep)},
            device_id_type=MESH,
        )

    def p_copy(k):
        span = pl.ds(k * group, group)
        return pltpu.make_async_remote_copy(
            src_ref=psend.at[span],
            dst_ref=precv.at[span],
            send_sem=psend_sem.at[k],
            recv_sem=precv_sem.at[k],
            device_id={"chan": outer},
            device_id_type=MESH,
        )

    def x_copy(o, p, incoming):
        block = lax.rem(s + n_seq - o, n_seq)
        which = lax.rem(r + n_rep - p, n_rep) if incoming else r
        place = wbuf.at[which, block]
        return pltpu.make_async_remote_copy(
            src_ref=place,
            dst_ref=place,
            send_sem=xsend_sem.at[o, p],
            recv_sem=xrecv_sem.at[o, p],
            device_id={"rep": lax.rem(r + p, n_rep)},
            device_id_type=MESH,
        )

    rate = decay_ref[...]
    amp = residue_ref[...] * jnp.sqrt(rate)
    step_of = lax.broadcasted_iota(jnp.int32, (STEP, ch), 0)
    for m in range(modes):
        t_out[m] = amp[m : m + 1] * jnp.exp(-rate[m : m + 1] * step_of.astype(F32))
    filt = t_out[0]
    for m in range(1, modes):
        filt = filt + t_out[m]
    for i in range(STEP):
        t_in[i] = jnp.exp(-rate * float(STEP - i))
        if i == 0:
            t_loc[i] = filt
        else:
            t_loc[i] = jnp.concatenate([jnp.zeros((i, ch), F32), filt[: STEP - i]], axis=0)
    acc[...] = jnp.zeros_like(acc)

    def multiply(block, span, h):
        def one(i, carry):
            off = pl.multiple_of(i * piece, piece)
            at = block * depth + off
            cols = pl.ds(pl.multiple_of(lax.rem(at, wdepth), piece), piece)
            outs = pl.ds(pl.multiple_of(h * half, 128), half)
            acc[span, outs] += lax.dot_general(
                tokbuf[block, span, pl.ds(off, piece)],
                wbuf[h, at // wdepth, :, cols],
                (((1,), (1,)), ((), ())),
                preferred_element_type=F32,
            )
            return carry

        lax.fori_loop(0, depth // piece, one, 0)

    own_tok.wait()
    for copy in own_w:
        copy.wait()

    reach = n_chan - 2 if proxied else n_chan - 1
    for d in range(1, n_chan - 1):
        for k in order:
            for way in range(2):
                block, there = source(way, d)

                @pl.when(there)
                def _():
                    tok_copy(block, k, way, False).wait_recv()

                    if d < reach:
                        @pl.when(can_send(way))
                        def _():
                            tok_copy(block, k, way, False).start()

        if d == 1 and proxied:
            @pl.when(at_end)
            def _():
                for q in range(wparts):
                    @pl.when(s != far)
                    def _():
                        w_copy(far_o, q, True).wait_recv()

                    f_copy(q).start()

    for o in range(1, n_seq):
        for q in range(wparts):
            if proxied:
                @pl.when(jnp.logical_not(at_end & (far_o == o)))
                def _():
                    w_copy(o, q, True).wait_recv()
            else:
                w_copy(o, q, True).wait_recv()
        for p in range(1, n_rep):
            x_copy(o, p, False).start()

    def early(h):
        def one(block, carry):
            off = block - c

            @pl.when((off < max(1, n_chan - 1)) & (off > -max(1, n_chan - 1)))
            def _():
                multiply(block, pl.ds(0, rows), h)

            return carry

        lax.fori_loop(0, n_chan, one, 0)

    def partial(h):
        def one(i, carry):
            cols = pl.ds(pl.multiple_of(i * piece, piece), piece)
            outs = pl.ds(pl.multiple_of(h * half, 128), half)
            pacc[:, outs] += lax.dot_general(
                tokbuf[far, :, cols],
                pbuf[h, :, cols],
                (((1,), (1,)), ((), ())),
                preferred_element_type=F32,
            )
            return carry

        lax.fori_loop(0, depth // piece, one, 0)

    early(r)
    if proxied:
        @pl.when(jnp.logical_not(at_end))
        def _():
            pacc[...] = jnp.zeros_like(pacc)
            for q in range(wparts):
                f_copy(q).wait_recv()
                for p in range(1, n_rep):
                    y_copy(p, q, False).start()
            partial(r)
            for p in range(1, n_rep):
                for q in range(wparts):
                    y_copy(p, q, True).wait_recv()
                partial(lax.rem(r + n_rep - p, n_rep))
            for k in order:
                span = pl.ds(k * group, group)
                psend[span, :] = pacc[span, :].astype(BF16)
                p_copy(k).start()
    for p in range(1, n_rep):
        for o in range(1, n_seq):
            x_copy(o, p, True).wait_recv()
        early(lax.rem(r + n_rep - p, n_rep))

    halo_copy = pltpu.make_async_remote_copy(
        src_ref=hsend,
        dst_ref=hrecv,
        send_sem=hsend_sem,
        recv_sem=hrecv_sem,
        device_id={"seq": lax.rem(s + 1, n_seq)},
        device_id_type=MESH,
    )
    skip = skip_ref[...]

    def first(b, carry):
        base = pl.multiple_of(b * STEP, STEP)
        feats = []
        for g in range(3):
            window = qbuf[pl.ds(base + 8, STEP + 8), g * ch : (g + 1) * ch]
            feat = taps_ref[0, g : g + 1] * window[8:]
            for j in range(1, 3):
                feat = feat + taps_ref[j, g : g + 1] * window[8 - j : 8 - j + STEP]
            feats.append(feat)
        z = (feats[1] * feats[2]).astype(BF16).astype(F32)
        query[pl.ds(base, STEP), :] = feats[0]
        grown = t_in[0] * z[0:1]
        total = skip * z + t_loc[0] * z[0:1]
        for i in range(1, STEP):
            grown = grown + t_in[i] * z[i : i + 1]
            total = total + t_loc[i] * z[i : i + 1]
        ubuf[b] = grown
        local[pl.ds(base, STEP), :] = total
        return carry

    per = group // STEP
    for k in order:
        span = pl.ds(k * group, group)
        if proxied:
            @pl.when(at_end)
            def _():
                p_copy(k).wait_recv()
                acc[span, :] += precv[span, :].astype(F32)
        elif n_chan > 1:
            for way in range(2):
                block, there = source(way, n_chan - 1)

                @pl.when(there)
                def _():
                    tok_copy(block, k, way, False).wait_recv()
                    for h in range(n_rep):
                        multiply(block, span, h)

        qbuf[HALO + k * group : HALO + (k + 1) * group, :] = acc[span, :].astype(BF16).astype(F32)
        if k == parts - 1:
            hsend[...] = qbuf[rows:, :].astype(BF16)

            @pl.when(s < n_seq - 1)
            def _():
                halo_copy.start()

            lax.fori_loop(k * per + 1, blocks, first, 0)
        else:
            if k == 0:
                @pl.when(s > 0)
                def _():
                    halo_copy.wait_recv()
                    qbuf[:HALO, :] = hrecv[...].astype(F32)

                @pl.when(s == 0)
                def _():
                    qbuf[:HALO, :] = jnp.zeros((HALO, 3 * ch), F32)

            lax.fori_loop(k * per, (k + 1) * per + (1 if k == parts - 2 else 0), first, 0)

    leap = jnp.exp(-rate * float(STEP))

    def scan(b, state):
        return leap * state + ubuf[b]

    ssend[...] = lax.fori_loop(0, blocks, scan, jnp.zeros((modes, ch), F32))

    def s_copy(o):
        return pltpu.make_async_remote_copy(
            src_ref=ssend,
            dst_ref=srecv.at[o],
            send_sem=ssend_sem.at[o],
            recv_sem=srecv_sem.at[o],
            device_id={"seq": lax.rem(s + o, n_seq)},
            device_id_type=MESH,
        )

    for o in range(1, n_seq):
        @pl.when(s + o < n_seq)
        def _():
            s_copy(o).start()

    acc2[:modes, :ch] = jnp.zeros((modes, ch), F32)
    for o in range(1, n_seq):
        @pl.when(s >= o)
        def _():
            s_copy(o).wait_recv()
            acc2[:modes, :ch] += jnp.exp(-rate * float(rows * (o - 1))) * srecv[o]

    def second(b, state):
        base = pl.multiple_of(b * STEP, STEP)
        total = local[pl.ds(base, STEP), :]
        for m in range(modes):
            total = total + t_out[m] * state[m : m + 1]
        longc = total.astype(BF16).astype(F32)
        gbuf[c, pl.ds(base, STEP), :] = (query[pl.ds(base, STEP), :] * longc).astype(BF16)
        return leap * state + ubuf[b]

    def g_copy(block, k, way):
        place = gbuf.at[block, pl.ds(k * group, group)]
        return pltpu.make_async_remote_copy(
            src_ref=place,
            dst_ref=place,
            send_sem=gsend_sem.at[way, block, k],
            recv_sem=grecv_sem.at[block, k],
            device_id={"chan": c + (1 if way == 0 else -1)},
            device_id_type=MESH,
        )

    state = acc2[:modes, :ch]
    for k in range(parts):
        state = lax.fori_loop(k * per, (k + 1) * per, second, state)
        for way in range(2):
            @pl.when(can_send(way))
            def _():
                g_copy(c, k, way).start()

    own_wout.wait()
    width = acc2.shape[1]
    tile = min(512, width)

    def project(block, opening):
        def one(i, carry):
            cols = pl.ds(pl.multiple_of(i * tile, tile), tile)
            part = jnp.dot(gbuf[block], woutbuf[block, :, cols], preferred_element_type=F32)
            if opening:
                acc2[:, cols] = part
            else:
                acc2[:, cols] += part
            return carry

        lax.fori_loop(0, width // tile, one, 0)

    project(c, True)
    for d in range(1, n_chan):
        for k in range(parts):
            for way in range(2):
                block, there = source(way, d)

                @pl.when(there)
                def _():
                    g_copy(block, k, way).wait_recv()

                    if d < n_chan - 1:
                        @pl.when(can_send(way))
                        def _():
                            g_copy(block, k, way).start()

        for e in range(1, n_chan - 1) if d == n_chan - 2 else [d] if d == n_chan - 1 else []:
            for way in range(2):
                block, there = source(way, e)

                @pl.when(there)
                def _():
                    project(block, False)

    out_ref[...] = acc2[...].astype(BF16)

    for d in range(n_chan - 1):
        for way in range(2):
            block, there = source(way, d)

            @pl.when(there & can_send(way))
            def _():
                for k in range(parts):
                    if d < reach:
                        tok_copy(block, k, way, d == 0).wait_send()
                    g_copy(block, k, way).wait_send()

    for o in range(1, n_seq):
        for q in range(wparts):
            w_copy(o, q, False).wait_send()
        for p in range(1, n_rep):
            x_copy(o, p, False).wait_send()

        @pl.when(s + o < n_seq)
        def _():
            s_copy(o).wait_send()

    if proxied:
        @pl.when(at_end)
        def _():
            for q in range(wparts):
                f_copy(q).wait_send()

        @pl.when(jnp.logical_not(at_end))
        def _():
            for q in range(wparts):
                for p in range(1, n_rep):
                    y_copy(p, q, False).wait_send()
            for k in range(parts):
                p_copy(k).wait_send()

    @pl.when(s < n_seq - 1)
    def _():
        halo_copy.wait_send()


def on_device(tokens, w_in, short_taps, decay, residue, skip, w_out):
    n_seq, n_chan, n_rep = (lax.axis_size(a) for a in ("seq", "chan", "rep"))
    rows, depth = tokens.shape
    ch, branches, wdepth = w_in.shape
    modes = decay.shape[0]
    width = w_out.shape[1]
    piece = min(512, depth, wdepth)
    parts = 4
    half = branches * ch // n_rep
    w = w_in.transpose(1, 0, 2).reshape(n_rep, half, wdepth)
    dims = (n_seq, n_chan, n_rep, parts, piece, rows, ch)
    vmem = pl.BlockSpec(memory_space=pltpu.VMEM)
    hbm = pl.BlockSpec(memory_space=pl.ANY)
    dma = pltpu.SemaphoreType.DMA
    return pl.pallas_call(
        functools.partial(kernel, dims),
        out_shape=jax.ShapeDtypeStruct((rows, width), BF16),
        in_specs=[hbm, hbm, vmem, vmem, vmem, vmem, hbm],
        out_specs=vmem,
        scratch_shapes=[
            pltpu.VMEM((n_chan, rows, depth), BF16),
            pltpu.VMEM((n_rep, n_seq, half, wdepth), BF16),
            pltpu.VMEM((n_chan, ch, width), BF16),
            pltpu.VMEM((rows, branches * ch), F32),
            pltpu.VMEM((rows + HALO, branches * ch), F32),
            pltpu.VMEM((HALO, branches * ch), BF16),
            pltpu.VMEM((HALO, branches * ch), BF16),
            pltpu.VMEM((rows, ch), F32),
            pltpu.VMEM((rows, ch), F32),
            pltpu.VMEM((rows // STEP, modes, ch), F32),
            pltpu.VMEM((modes, ch), F32),
            pltpu.VMEM((n_seq, modes, ch), F32),
            pltpu.VMEM((STEP, modes, ch), F32),
            pltpu.VMEM((modes, STEP, ch), F32),
            pltpu.VMEM((STEP, STEP, ch), F32),
            pltpu.VMEM((n_chan, rows, ch), BF16),
            pltpu.VMEM((rows, width), F32),
            pltpu.VMEM((n_rep, half, wdepth), BF16),
            pltpu.VMEM((rows, branches * ch), F32),
            pltpu.VMEM((rows, branches * ch), BF16),
            pltpu.VMEM((rows, branches * ch), BF16),
            dma((2 + n_rep,)),
            dma((2, n_chan, parts)),
            dma((n_chan, parts)),
            dma((n_seq, 4)),
            dma((n_seq, 4)),
            dma((n_seq, n_rep)),
            dma((n_seq, n_rep)),
            dma((4,)),
            dma((4,)),
            dma((n_rep, 4)),
            dma((n_rep, 4)),
            dma((parts,)),
            dma((parts,)),
            dma(()),
            dma(()),
            dma((n_seq,)),
            dma((n_seq,)),
            dma((2, n_chan, parts)),
            dma((n_chan, parts)),
        ],
        compiler_params=pltpu.CompilerParams(
            collective_id=0, has_side_effects=True, vmem_limit_bytes=56 * 1024 * 1024
        ),
        cost_estimate=pl.CostEstimate(
            flops=2 * rows * (n_chan * depth * branches * ch + n_chan * ch * width),
            bytes_accessed=2 * (rows * depth + branches * ch * wdepth + n_chan * ch * width),
            transcendentals=0,
        ),
    )(tokens, w, short_taps, decay, residue, skip.reshape(1, ch), w_out.reshape(n_chan, ch, width))


def solution(mesh):
    placed = (
        P(("rep", "seq"), "chan"),
        P("chan", None, "seq"),
        P(None, None, "chan"),
        P(None, "chan"),
        P(None, "chan"),
        P("chan"),
        P(None, "chan"),
    )
    return jax.shard_map(
        on_device, mesh=mesh, in_specs=placed, out_specs=P(("rep", "seq"), "chan"), check_vma=False
    )
```

```python
import functools

import jax
import jax.numpy as jnp
from jax import lax
from jax.experimental import pallas as pl
from jax.experimental.pallas import tpu as pltpu
from jax.sharding import PartitionSpec as P

MESH = pl.DeviceIdType.MESH
F32 = jnp.float32
BF16 = jnp.bfloat16
STEP = 16
HALO = 16


def kernel(
    dims,
    tok_hbm, w_hbm, taps_ref, decay_ref, residue_ref, skip_ref, wout_hbm,
    out_ref,
    tokbuf, wbuf, woutbuf, acc, qbuf, hsend, hrecv, local, query, ubuf, ssend, srecv,
    t_in, t_out, t_loc, gbuf, acc2, pbuf, pacc, psend, precv,
    loc_sem, tsend_sem, trecv_sem, wsend_sem, wrecv_sem, xsend_sem, xrecv_sem,
    fsend_sem, frecv_sem, ysend_sem, yrecv_sem, psend_sem, precv_sem,
    hsend_sem, hrecv_sem, ssend_sem, srecv_sem, gsend_sem, grecv_sem,
):
    n_seq, n_chan, n_rep, parts, piece, rows, ch = dims
    modes = decay_ref.shape[0]
    half, wdepth = wbuf.shape[2:]
    depth = tokbuf.shape[2]
    group = rows // parts
    proxied = n_chan == 4 and n_seq == n_chan and depth == wdepth
    wparts = 4 if proxied else 1
    wpiece = wdepth // wparts
    order = [parts - 1] + list(range(parts - 1))
    s = lax.axis_index("seq")
    c = lax.axis_index("chan")
    r = lax.axis_index("rep")
    blocks = rows // STEP

    barrier = pltpu.get_barrier_semaphore()
    for o in range(1, n_seq):
        pl.semaphore_signal(
            barrier, inc=1, device_id={"seq": lax.rem(s + o, n_seq)}, device_id_type=MESH
        )
    for o in range(1, n_rep):
        pl.semaphore_signal(
            barrier, inc=1, device_id={"rep": lax.rem(r + o, n_rep)}, device_id_type=MESH
        )

    @pl.when(c > 0)
    def _():
        pl.semaphore_signal(barrier, inc=1, device_id={"chan": c - 1}, device_id_type=MESH)

    @pl.when(c < n_chan - 1)
    def _():
        pl.semaphore_signal(barrier, inc=1, device_id={"chan": c + 1}, device_id_type=MESH)

    own_tok = pltpu.make_async_copy(tok_hbm, tokbuf.at[c], loc_sem.at[0])
    own_w = [
        pltpu.make_async_copy(w_hbm.at[h], wbuf.at[h, s], loc_sem.at[2 + h]) for h in range(n_rep)
    ]
    own_wout = pltpu.make_async_copy(wout_hbm, woutbuf, loc_sem.at[1])
    own_tok.start()
    for copy in own_w:
        copy.start()
    own_wout.start()

    peers = n_seq - 1 + n_rep - 1
    at_end = (c == 0) | (c == n_chan - 1)

    @pl.when(at_end)
    def _():
        pl.semaphore_wait(barrier, peers + min(1, n_chan - 1))

    @pl.when(jnp.logical_not(at_end))
    def _():
        pl.semaphore_wait(barrier, peers + 2)

    def tok_copy(block, k, way, own):
        span = pl.ds(k * group, group)
        return pltpu.make_async_remote_copy(
            src_ref=tok_hbm.at[span] if own else tokbuf.at[block, span],
            dst_ref=tokbuf.at[block, span],
            send_sem=tsend_sem.at[way, block, k],
            recv_sem=trecv_sem.at[block, k],
            device_id={"chan": c + (1 if way == 0 else -1)},
            device_id_type=MESH,
        )

    def can_send(way):
        return c < n_chan - 1 if way == 0 else c > 0

    def source(way, d):
        block = c - d if way == 0 else c + d
        there = block >= 0 if way == 0 else block <= n_chan - 1
        return block, there

    for k in order:
        for way in range(2):
            @pl.when(can_send(way))
            def _():
                tok_copy(c, k, way, True).start()

    def partner(o):
        if proxied:
            flips = (s + 1 - 2 * lax.rem(s, 2), s + 2 - 4 * (s // 2), 3 - s)
            return flips[abs(o) - 1]
        return lax.rem(s + n_seq + o, n_seq)

    def relay(q):
        place = wbuf.at[r, partner(1 + q % 2), :, pl.ds(q * wpiece, wpiece)]
        return pltpu.make_async_remote_copy(
            src_ref=place,
            dst_ref=place,
            send_sem=wsend_sem.at[3, q],
            recv_sem=wrecv_sem.at[3, q],
            device_id={"seq": partner(2 - q % 2)},
            device_id_type=MESH,
        )

    def w_copy(o, q, incoming):
        cols = pl.ds(q * wpiece, wpiece)
        to = partner(o)
        block = partner(-o) if incoming else s
        return pltpu.make_async_remote_copy(
            src_ref=w_hbm.at[r, :, cols],
            dst_ref=wbuf.at[r, block, :, cols],
            send_sem=wsend_sem.at[o, q],
            recv_sem=wrecv_sem.at[o, q],
            device_id={"seq": to},
            device_id_type=MESH,
        )

    for q in range(wparts):
        for o in range(1, 3 if proxied else n_seq):
            w_copy(o, q, False).start()

    at_low = c == 0
    far = jnp.where(c < n_chan // 2, n_chan - 1, 0)
    late = at_end & (s + far == 3)
    inner = jnp.where(at_low, c + 1, c - 1)
    outer = jnp.where(c == 1, c - 1, c + 1)

    def f_copy(q):
        cols = pl.ds(q * wpiece, wpiece)
        return pltpu.make_async_remote_copy(
            src_ref=wbuf.at[r, far, :, cols],
            dst_ref=pbuf.at[r, :, cols],
            send_sem=fsend_sem.at[q],
            recv_sem=frecv_sem.at[q],
            device_id={"chan": inner},
            device_id_type=MESH,
        )

    def y_copy(p, q, incoming):
        which = lax.rem(r + n_rep - p, n_rep) if incoming else r
        place = pbuf.at[which, :, pl.ds(q * wpiece, wpiece)]
        return pltpu.make_async_remote_copy(
            src_ref=place,
            dst_ref=place,
            send_sem=ysend_sem.at[p, q],
            recv_sem=yrecv_sem.at[p, q],
            device_id={"rep": lax.rem(r + p, n_rep)},
            device_id_type=MESH,
        )

    def p_copy(k):
        span = pl.ds(k * group, group)
        return pltpu.make_async_remote_copy(
            src_ref=psend.at[span],
            dst_ref=precv.at[span],
            send_sem=psend_sem.at[k],
            recv_sem=precv_sem.at[k],
            device_id={"chan": outer},
            device_id_type=MESH,
        )

    def x_copy(o, p, incoming):
        block = partner(-o)
        which = lax.rem(r + n_rep - p, n_rep) if incoming else r
        place = wbuf.at[which, block]
        return pltpu.make_async_remote_copy(
            src_ref=place,
            dst_ref=place,
            send_sem=xsend_sem.at[o, p],
            recv_sem=xrecv_sem.at[o, p],
            device_id={"rep": lax.rem(r + p, n_rep)},
            device_id_type=MESH,
        )

    rate = decay_ref[...]
    amp = residue_ref[...] * jnp.sqrt(rate)
    step_of = lax.broadcasted_iota(jnp.int32, (STEP, ch), 0)
    for m in range(modes):
        t_out[m] = amp[m : m + 1] * jnp.exp(-rate[m : m + 1] * step_of.astype(F32))
    filt = t_out[0]
    for m in range(1, modes):
        filt = filt + t_out[m]
    for i in range(STEP):
        t_in[i] = jnp.exp(-rate * float(STEP - i))
        if i == 0:
            t_loc[i] = filt
        else:
            t_loc[i] = jnp.concatenate([jnp.zeros((i, ch), F32), filt[: STEP - i]], axis=0)
    acc[...] = jnp.zeros_like(acc)

    def multiply(block, span, h):
        def one(i, carry):
            off = pl.multiple_of(i * piece, piece)
            at = block * depth + off
            cols = pl.ds(pl.multiple_of(lax.rem(at, wdepth), piece), piece)
            outs = pl.ds(pl.multiple_of(h * half, 128), half)
            acc[span, outs] += lax.dot_general(
                tokbuf[block, span, pl.ds(off, piece)],
                wbuf[h, at // wdepth, :, cols],
                (((1,), (1,)), ((), ())),
                preferred_element_type=F32,
            )
            return carry

        lax.fori_loop(0, depth // piece, one, 0)

    own_tok.wait()
    for copy in own_w:
        copy.wait()

    reach = n_chan - 2 if proxied else n_chan - 1
    for d in range(1, n_chan - 1):
        for k in order:
            for way in range(2):
                block, there = source(way, d)

                @pl.when(there)
                def _():
                    tok_copy(block, k, way, False).wait_recv()

                    if d < reach:
                        @pl.when(can_send(way))
                        def _():
                            tok_copy(block, k, way, False).start()

            if d == 1 and proxied:
                q = order.index(k)
                w_copy(1, q, True).wait_recv()
                w_copy(2, q, True).wait_recv()
                relay(q).start()

                @pl.when(at_end & jnp.logical_not(late))
                def _():
                    f_copy(q).start()

        if d == 1 and proxied:
            @pl.when(late)
            def _():
                for q in range(wparts):
                    w_copy(3, q, True).wait_recv()
                    f_copy(q).start()

    for o in range(1, n_seq):
        for q in range(wparts):
            if proxied:
                if o == 3:
                    @pl.when(jnp.logical_not(late))
                    def _():
                        w_copy(o, q, True).wait_recv()
            else:
                w_copy(o, q, True).wait_recv()
        for p in range(1, n_rep):
            x_copy(o, p, False).start()

    def early(h):
        def one(block, carry):
            off = block - c

            @pl.when((off < max(1, n_chan - 1)) & (off > -max(1, n_chan - 1)))
            def _():
                multiply(block, pl.ds(0, rows), h)

            return carry

        lax.fori_loop(0, n_chan, one, 0)

    def partial(h):
        def one(i, carry):
            cols = pl.ds(pl.multiple_of(i * piece, piece), piece)
            outs = pl.ds(pl.multiple_of(h * half, 128), half)
            pacc[:, outs] += lax.dot_general(
                tokbuf[far, :, cols],
                pbuf[h, :, cols],
                (((1,), (1,)), ((), ())),
                preferred_element_type=F32,
            )
            return carry

        lax.fori_loop(0, depth // piece, one, 0)

    early(r)
    if proxied:
        @pl.when(jnp.logical_not(at_end))
        def _():
            pacc[...] = jnp.zeros_like(pacc)
            for q in range(wparts):
                f_copy(q).wait_recv()
                for p in range(1, n_rep):
                    y_copy(p, q, False).start()
            partial(r)
            for p in range(1, n_rep):
                for q in range(wparts):
                    y_copy(p, q, True).wait_recv()
                partial(lax.rem(r + n_rep - p, n_rep))
            for k in order:
                span = pl.ds(k * group, group)
                psend[span, :] = pacc[span, :].astype(BF16)
                p_copy(k).start()
    for p in range(1, n_rep):
        for o in range(1, n_seq):
            x_copy(o, p, True).wait_recv()
        early(lax.rem(r + n_rep - p, n_rep))

    halo_copy = pltpu.make_async_remote_copy(
        src_ref=hsend,
        dst_ref=hrecv,
        send_sem=hsend_sem,
        recv_sem=hrecv_sem,
        device_id={"seq": lax.rem(s + 1, n_seq)},
        device_id_type=MESH,
    )
    skip = skip_ref[...]

    def first(b, carry):
        base = pl.multiple_of(b * STEP, STEP)
        feats = []
        for g in range(3):
            window = qbuf[pl.ds(base + 8, STEP + 8), g * ch : (g + 1) * ch]
            feat = taps_ref[0, g : g + 1] * window[8:]
            for j in range(1, 3):
                feat = feat + taps_ref[j, g : g + 1] * window[8 - j : 8 - j + STEP]
            feats.append(feat)
        z = (feats[1] * feats[2]).astype(BF16).astype(F32)
        query[pl.ds(base, STEP), :] = feats[0]
        grown = t_in[0] * z[0:1]
        total = skip * z + t_loc[0] * z[0:1]
        for i in range(1, STEP):
            grown = grown + t_in[i] * z[i : i + 1]
            total = total + t_loc[i] * z[i : i + 1]
        ubuf[b] = grown
        local[pl.ds(base, STEP), :] = total
        return carry

    per = group // STEP
    for k in order:
        span = pl.ds(k * group, group)
        if proxied:
            @pl.when(at_end)
            def _():
                p_copy(k).wait_recv()
                acc[span, :] += precv[span, :].astype(F32)
        elif n_chan > 1:
            for way in range(2):
                block, there = source(way, n_chan - 1)

                @pl.when(there)
                def _():
                    tok_copy(block, k, way, False).wait_recv()
                    for h in range(n_rep):
                        multiply(block, span, h)

        qbuf[HALO + k * group : HALO + (k + 1) * group, :] = acc[span, :].astype(BF16).astype(F32)
        if k == parts - 1:
            hsend[...] = qbuf[rows:, :].astype(BF16)

            @pl.when(s < n_seq - 1)
            def _():
                halo_copy.start()

            lax.fori_loop(k * per + 1, blocks, first, 0)
        else:
            if k == 0:
                @pl.when(s > 0)
                def _():
                    halo_copy.wait_recv()
                    qbuf[:HALO, :] = hrecv[...].astype(F32)

                @pl.when(s == 0)
                def _():
                    qbuf[:HALO, :] = jnp.zeros((HALO, 3 * ch), F32)

            lax.fori_loop(k * per, (k + 1) * per + (1 if k == parts - 2 else 0), first, 0)

    leap = jnp.exp(-rate * float(STEP))

    def scan(b, state):
        return leap * state + ubuf[b]

    ssend[...] = lax.fori_loop(0, blocks, scan, jnp.zeros((modes, ch), F32))

    def s_copy(o):
        return pltpu.make_async_remote_copy(
            src_ref=ssend,
            dst_ref=srecv.at[o],
            send_sem=ssend_sem.at[o],
            recv_sem=srecv_sem.at[o],
            device_id={"seq": lax.rem(s + o, n_seq)},
            device_id_type=MESH,
        )

    for o in range(1, n_seq):
        @pl.when(s + o < n_seq)
        def _():
            s_copy(o).start()

    acc2[:modes, :ch] = jnp.zeros((modes, ch), F32)
    for o in range(1, n_seq):
        @pl.when(s >= o)
        def _():
            s_copy(o).wait_recv()
            acc2[:modes, :ch] += jnp.exp(-rate * float(rows * (o - 1))) * srecv[o]

    def second(b, state):
        base = pl.multiple_of(b * STEP, STEP)
        total = local[pl.ds(base, STEP), :]
        for m in range(modes):
            total = total + t_out[m] * state[m : m + 1]
        longc = total.astype(BF16).astype(F32)
        gbuf[c, pl.ds(base, STEP), :] = (query[pl.ds(base, STEP), :] * longc).astype(BF16)
        return leap * state + ubuf[b]

    def g_copy(block, k, way):
        place = gbuf.at[block, pl.ds(k * group, group)]
        return pltpu.make_async_remote_copy(
            src_ref=place,
            dst_ref=place,
            send_sem=gsend_sem.at[way, block, k],
            recv_sem=grecv_sem.at[block, k],
            device_id={"chan": c + (1 if way == 0 else -1)},
            device_id_type=MESH,
        )

    state = acc2[:modes, :ch]
    for k in range(parts):
        state = lax.fori_loop(k * per, (k + 1) * per, second, state)
        for way in range(2):
            @pl.when(can_send(way))
            def _():
                g_copy(c, k, way).start()

    own_wout.wait()
    width = acc2.shape[1]
    tile = min(512, width)

    def project(block, opening):
        def one(i, carry):
            cols = pl.ds(pl.multiple_of(i * tile, tile), tile)
            part = jnp.dot(gbuf[block], woutbuf[block, :, cols], preferred_element_type=F32)
            if opening:
                acc2[:, cols] = part
            else:
                acc2[:, cols] += part
            return carry

        lax.fori_loop(0, width // tile, one, 0)

    project(c, True)
    for d in range(1, n_chan):
        for k in range(parts):
            for way in range(2):
                block, there = source(way, d)

                @pl.when(there)
                def _():
                    g_copy(block, k, way).wait_recv()

                    if d < n_chan - 1:
                        @pl.when(can_send(way))
                        def _():
                            g_copy(block, k, way).start()

        for e in range(1, n_chan - 1) if d == n_chan - 2 else [d] if d == n_chan - 1 else []:
            for way in range(2):
                block, there = source(way, e)

                @pl.when(there)
                def _():
                    project(block, False)

    out_ref[...] = acc2[...].astype(BF16)

    for d in range(n_chan - 1):
        for way in range(2):
            block, there = source(way, d)

            @pl.when(there & can_send(way))
            def _():
                for k in range(parts):
                    if d < reach:
                        tok_copy(block, k, way, d == 0).wait_send()
                    g_copy(block, k, way).wait_send()

    for o in range(1, n_seq):
        for q in range(wparts):
            (relay(q) if proxied and o == 3 else w_copy(o, q, False)).wait_send()
        for p in range(1, n_rep):
            x_copy(o, p, False).wait_send()

        @pl.when(s + o < n_seq)
        def _():
            s_copy(o).wait_send()

    if proxied:
        @pl.when(at_end)
        def _():
            for q in range(wparts):
                f_copy(q).wait_send()

        @pl.when(jnp.logical_not(at_end))
        def _():
            for q in range(wparts):
                for p in range(1, n_rep):
                    y_copy(p, q, False).wait_send()
            for k in range(parts):
                p_copy(k).wait_send()

    @pl.when(s < n_seq - 1)
    def _():
        halo_copy.wait_send()


def on_device(tokens, w_in, short_taps, decay, residue, skip, w_out):
    n_seq, n_chan, n_rep = (lax.axis_size(a) for a in ("seq", "chan", "rep"))
    rows, depth = tokens.shape
    ch, branches, wdepth = w_in.shape
    modes = decay.shape[0]
    width = w_out.shape[1]
    piece = min(512, depth, wdepth)
    parts = 4
    half = branches * ch // n_rep
    w = w_in.transpose(1, 0, 2).reshape(n_rep, half, wdepth)
    dims = (n_seq, n_chan, n_rep, parts, piece, rows, ch)
    vmem = pl.BlockSpec(memory_space=pltpu.VMEM)
    hbm = pl.BlockSpec(memory_space=pl.ANY)
    dma = pltpu.SemaphoreType.DMA
    return pl.pallas_call(
        functools.partial(kernel, dims),
        out_shape=jax.ShapeDtypeStruct((rows, width), BF16),
        in_specs=[hbm, hbm, vmem, vmem, vmem, vmem, hbm],
        out_specs=vmem,
        scratch_shapes=[
            pltpu.VMEM((n_chan, rows, depth), BF16),
            pltpu.VMEM((n_rep, n_seq, half, wdepth), BF16),
            pltpu.VMEM((n_chan, ch, width), BF16),
            pltpu.VMEM((rows, branches * ch), F32),
            pltpu.VMEM((rows + HALO, branches * ch), F32),
            pltpu.VMEM((HALO, branches * ch), BF16),
            pltpu.VMEM((HALO, branches * ch), BF16),
            pltpu.VMEM((rows, ch), F32),
            pltpu.VMEM((rows, ch), F32),
            pltpu.VMEM((rows // STEP, modes, ch), F32),
            pltpu.VMEM((modes, ch), F32),
            pltpu.VMEM((n_seq, modes, ch), F32),
            pltpu.VMEM((STEP, modes, ch), F32),
            pltpu.VMEM((modes, STEP, ch), F32),
            pltpu.VMEM((STEP, STEP, ch), F32),
            pltpu.VMEM((n_chan, rows, ch), BF16),
            pltpu.VMEM((rows, width), F32),
            pltpu.VMEM((n_rep, half, wdepth), BF16),
            pltpu.VMEM((rows, branches * ch), F32),
            pltpu.VMEM((rows, branches * ch), BF16),
            pltpu.VMEM((rows, branches * ch), BF16),
            dma((2 + n_rep,)),
            dma((2, n_chan, parts)),
            dma((n_chan, parts)),
            dma((n_seq, 4)),
            dma((n_seq, 4)),
            dma((n_seq, n_rep)),
            dma((n_seq, n_rep)),
            dma((4,)),
            dma((4,)),
            dma((n_rep, 4)),
            dma((n_rep, 4)),
            dma((parts,)),
            dma((parts,)),
            dma(()),
            dma(()),
            dma((n_seq,)),
            dma((n_seq,)),
            dma((2, n_chan, parts)),
            dma((n_chan, parts)),
        ],
        compiler_params=pltpu.CompilerParams(
            collective_id=0, has_side_effects=True, vmem_limit_bytes=56 * 1024 * 1024
        ),
        cost_estimate=pl.CostEstimate(
            flops=2 * rows * (n_chan * depth * branches * ch + n_chan * ch * width),
            bytes_accessed=2 * (rows * depth + branches * ch * wdepth + n_chan * ch * width),
            transcendentals=0,
        ),
    )(tokens, w, short_taps, decay, residue, skip.reshape(1, ch), w_out.reshape(n_chan, ch, width))


def solution(mesh):
    placed = (
        P(("rep", "seq"), "chan"),
        P("chan", None, "seq"),
        P(None, None, "chan"),
        P(None, "chan"),
        P(None, "chan"),
        P("chan"),
        P(None, "chan"),
    )
    return jax.shard_map(
        on_device, mesh=mesh, in_specs=placed, out_specs=P(("rep", "seq"), "chan"), check_vma=False
    )
```

```python
import functools

import jax
import jax.numpy as jnp
from jax import lax
from jax.experimental import pallas as pl
from jax.experimental.pallas import tpu as pltpu
from jax.sharding import PartitionSpec as P

MESH = pl.DeviceIdType.MESH
F32 = jnp.float32
BF16 = jnp.bfloat16
STEP = 16
HALO = 16


def kernel(
    dims,
    tok_hbm, w_hbm, taps_ref, decay_ref, residue_ref, skip_ref, wout_hbm,
    out_ref,
    tokbuf, wbuf, woutbuf, acc, qbuf, hsend, hrecv, local, query, ubuf, ssend, srecv,
    t_in, t_out, t_loc, gbuf, acc2, pbuf, pacc, psend, precv,
    loc_sem, tsend_sem, trecv_sem, wsend_sem, wrecv_sem, xsend_sem, xrecv_sem,
    fsend_sem, frecv_sem, ysend_sem, yrecv_sem, psend_sem, precv_sem,
    hsend_sem, hrecv_sem, ssend_sem, srecv_sem, gsend_sem, grecv_sem,
):
    n_seq, n_chan, n_rep, parts, piece, rows, ch = dims
    modes = decay_ref.shape[0]
    half, wdepth = wbuf.shape[2:]
    depth = tokbuf.shape[2]
    group = rows // parts
    proxied = n_chan == 4 and n_seq == n_chan and depth == wdepth
    wparts = 4 if proxied else 1
    wpiece = wdepth // wparts
    order = [parts - 1] + list(range(parts - 1))
    s = lax.axis_index("seq")
    c = lax.axis_index("chan")
    r = lax.axis_index("rep")
    blocks = rows // STEP

    barrier = pltpu.get_barrier_semaphore()
    for o in range(1, n_seq):
        pl.semaphore_signal(
            barrier, inc=1, device_id={"seq": lax.rem(s + o, n_seq)}, device_id_type=MESH
        )
    for o in range(1, n_rep):
        pl.semaphore_signal(
            barrier, inc=1, device_id={"rep": lax.rem(r + o, n_rep)}, device_id_type=MESH
        )

    @pl.when(c > 0)
    def _():
        pl.semaphore_signal(barrier, inc=1, device_id={"chan": c - 1}, device_id_type=MESH)

    @pl.when(c < n_chan - 1)
    def _():
        pl.semaphore_signal(barrier, inc=1, device_id={"chan": c + 1}, device_id_type=MESH)

    own_tok = pltpu.make_async_copy(tok_hbm, tokbuf.at[c], loc_sem.at[0])
    own_w = [
        pltpu.make_async_copy(w_hbm.at[h], wbuf.at[h, s], loc_sem.at[2 + h]) for h in range(n_rep)
    ]
    own_wout = pltpu.make_async_copy(wout_hbm, woutbuf, loc_sem.at[1])
    own_tok.start()
    for copy in own_w:
        copy.start()
    own_wout.start()

    peers = n_seq - 1 + n_rep - 1
    at_end = (c == 0) | (c == n_chan - 1)

    @pl.when(at_end)
    def _():
        pl.semaphore_wait(barrier, peers + min(1, n_chan - 1))

    @pl.when(jnp.logical_not(at_end))
    def _():
        pl.semaphore_wait(barrier, peers + 2)

    def tok_copy(block, k, way, own):
        span = pl.ds(k * group, group)
        return pltpu.make_async_remote_copy(
            src_ref=tok_hbm.at[span] if own else tokbuf.at[block, span],
            dst_ref=tokbuf.at[block, span],
            send_sem=tsend_sem.at[way, block, k],
            recv_sem=trecv_sem.at[block, k],
            device_id={"chan": c + (1 if way == 0 else -1)},
            device_id_type=MESH,
        )

    def can_send(way):
        return c < n_chan - 1 if way == 0 else c > 0

    def source(way, d):
        block = c - d if way == 0 else c + d
        there = block >= 0 if way == 0 else block <= n_chan - 1
        return block, there

    for k in order:
        for way in range(2):
            @pl.when(can_send(way))
            def _():
                tok_copy(c, k, way, True).start()

    def partner(o):
        if proxied:
            flips = (s + 1 - 2 * lax.rem(s, 2), s + 2 - 4 * (s // 2), 3 - s)
            return flips[abs(o) - 1]
        return lax.rem(s + n_seq + o, n_seq)

    def relay(q):
        place = wbuf.at[r, partner(1 + q % 2), :, pl.ds(q * wpiece, wpiece)]
        return pltpu.make_async_remote_copy(
            src_ref=place,
            dst_ref=place,
            send_sem=wsend_sem.at[3, q],
            recv_sem=wrecv_sem.at[3, q],
            device_id={"seq": partner(2 - q % 2)},
            device_id_type=MESH,
        )

    def w_copy(o, q, incoming):
        cols = pl.ds(q * wpiece, wpiece)
        to = partner(o)
        block = partner(-o) if incoming else s
        return pltpu.make_async_remote_copy(
            src_ref=w_hbm.at[r, :, cols],
            dst_ref=wbuf.at[r, block, :, cols],
            send_sem=wsend_sem.at[o, q],
            recv_sem=wrecv_sem.at[o, q],
            device_id={"seq": to},
            device_id_type=MESH,
        )

    for q in range(wparts):
        for o in range(1, 3 if proxied else n_seq):
            w_copy(o, q, False).start()

    at_low = c == 0
    far = jnp.where(c < n_chan // 2, n_chan - 1, 0)
    late = at_end & (s + far == 3)
    inner = jnp.where(at_low, c + 1, c - 1)
    outer = jnp.where(c == 1, c - 1, c + 1)

    def f_copy(q):
        cols = pl.ds(q * wpiece, wpiece)
        return pltpu.make_async_remote_copy(
            src_ref=wbuf.at[r, far, :, cols],
            dst_ref=pbuf.at[r, :, cols],
            send_sem=fsend_sem.at[q],
            recv_sem=frecv_sem.at[q],
            device_id={"chan": inner},
            device_id_type=MESH,
        )

    def y_copy(p, q, incoming):
        which = lax.rem(r + n_rep - p, n_rep) if incoming else r
        place = pbuf.at[which, :, pl.ds(q * wpiece, wpiece)]
        return pltpu.make_async_remote_copy(
            src_ref=place,
            dst_ref=place,
            send_sem=ysend_sem.at[p, q],
            recv_sem=yrecv_sem.at[p, q],
            device_id={"rep": lax.rem(r + p, n_rep)},
            device_id_type=MESH,
        )

    def p_copy(k):
        span = pl.ds(k * group, group)
        return pltpu.make_async_remote_copy(
            src_ref=psend.at[span],
            dst_ref=precv.at[span],
            send_sem=psend_sem.at[k],
            recv_sem=precv_sem.at[k],
            device_id={"chan": outer},
            device_id_type=MESH,
        )

    def x_copy(o, p, incoming):
        block = partner(-o)
        which = lax.rem(r + n_rep - p, n_rep) if incoming else r
        place = wbuf.at[which, block]
        return pltpu.make_async_remote_copy(
            src_ref=place,
            dst_ref=place,
            send_sem=xsend_sem.at[o, p],
            recv_sem=xrecv_sem.at[o, p],
            device_id={"rep": lax.rem(r + p, n_rep)},
            device_id_type=MESH,
        )

    rate = decay_ref[...]
    amp = residue_ref[...] * jnp.sqrt(rate)
    step_of = lax.broadcasted_iota(jnp.int32, (STEP, ch), 0)
    for m in range(modes):
        t_out[m] = amp[m : m + 1] * jnp.exp(-rate[m : m + 1] * step_of.astype(F32))
    filt = t_out[0]
    for m in range(1, modes):
        filt = filt + t_out[m]
    for i in range(STEP):
        t_in[i] = jnp.exp(-rate * float(STEP - i))
        if i == 0:
            t_loc[i] = filt
        else:
            t_loc[i] = jnp.concatenate([jnp.zeros((i, ch), F32), filt[: STEP - i]], axis=0)
    acc[...] = jnp.zeros_like(acc)

    def multiply(block, span, h):
        def one(i, carry):
            off = pl.multiple_of(i * piece, piece)
            at = block * depth + off
            cols = pl.ds(pl.multiple_of(lax.rem(at, wdepth), piece), piece)
            outs = pl.ds(pl.multiple_of(h * half, 128), half)
            acc[span, outs] += lax.dot_general(
                tokbuf[block, span, pl.ds(off, piece)],
                wbuf[h, at // wdepth, :, cols],
                (((1,), (1,)), ((), ())),
                preferred_element_type=F32,
            )
            return carry

        lax.fori_loop(0, depth // piece, one, 0)

    own_tok.wait()
    for copy in own_w:
        copy.wait()

    reach = n_chan - 2 if proxied else n_chan - 1
    for d in range(1, n_chan - 1):
        for k in order:
            for way in range(2):
                block, there = source(way, d)

                @pl.when(there)
                def _():
                    tok_copy(block, k, way, False).wait_recv()

                    if d < reach:
                        @pl.when(can_send(way))
                        def _():
                            tok_copy(block, k, way, False).start()

            if d == 1 and proxied:
                q = order.index(k)
                w_copy(1, q, True).wait_recv()
                w_copy(2, q, True).wait_recv()
                relay(q).start()

                @pl.when(at_end & jnp.logical_not(late))
                def _():
                    f_copy(q).start()

        if d == 1 and proxied:
            @pl.when(late)
            def _():
                for q in range(wparts):
                    w_copy(3, q, True).wait_recv()
                    f_copy(q).start()

    for o in range(1, n_seq):
        for q in range(wparts):
            if proxied:
                if o == 3:
                    @pl.when(jnp.logical_not(late))
                    def _():
                        w_copy(o, q, True).wait_recv()
            else:
                w_copy(o, q, True).wait_recv()
        for p in range(1, n_rep):
            x_copy(o, p, False).start()

    def early(h):
        def one(block, carry):
            off = block - c

            @pl.when((off < max(1, n_chan - 1)) & (off > -max(1, n_chan - 1)))
            def _():
                multiply(block, pl.ds(0, rows), h)

            return carry

        lax.fori_loop(0, n_chan, one, 0)

    def partial(h):
        def one(i, carry):
            cols = pl.ds(pl.multiple_of(i * piece, piece), piece)
            outs = pl.ds(pl.multiple_of(h * half, 128), half)
            pacc[:, outs] += lax.dot_general(
                tokbuf[far, :, cols],
                pbuf[h, :, cols],
                (((1,), (1,)), ((), ())),
                preferred_element_type=F32,
            )
            return carry

        lax.fori_loop(0, depth // piece, one, 0)

    if proxied:
        @pl.when(jnp.logical_not(at_end))
        def _():
            pacc[...] = jnp.zeros_like(pacc)
            for q in range(wparts):
                f_copy(q).wait_recv()
                for p in range(1, n_rep):
                    y_copy(p, q, False).start()
            partial(r)
            for p in range(1, n_rep):
                for q in range(wparts):
                    y_copy(p, q, True).wait_recv()
                partial(lax.rem(r + n_rep - p, n_rep))
            for k in order:
                span = pl.ds(k * group, group)
                psend[span, :] = pacc[span, :].astype(BF16)
                p_copy(k).start()

    early(r)
    for p in range(1, n_rep):
        for o in range(1, n_seq):
            x_copy(o, p, True).wait_recv()
        early(lax.rem(r + n_rep - p, n_rep))

    halo_copy = pltpu.make_async_remote_copy(
        src_ref=hsend,
        dst_ref=hrecv,
        send_sem=hsend_sem,
        recv_sem=hrecv_sem,
        device_id={"seq": lax.rem(s + 1, n_seq)},
        device_id_type=MESH,
    )
    skip = skip_ref[...]

    def first(b, carry):
        base = pl.multiple_of(b * STEP, STEP)
        feats = []
        for g in range(3):
            window = qbuf[pl.ds(base + 8, STEP + 8), g * ch : (g + 1) * ch]
            feat = taps_ref[0, g : g + 1] * window[8:]
            for j in range(1, 3):
                feat = feat + taps_ref[j, g : g + 1] * window[8 - j : 8 - j + STEP]
            feats.append(feat)
        z = (feats[1] * feats[2]).astype(BF16).astype(F32)
        query[pl.ds(base, STEP), :] = feats[0]
        grown = t_in[0] * z[0:1]
        total = skip * z + t_loc[0] * z[0:1]
        for i in range(1, STEP):
            grown = grown + t_in[i] * z[i : i + 1]
            total = total + t_loc[i] * z[i : i + 1]
        ubuf[b] = grown
        local[pl.ds(base, STEP), :] = total
        return carry

    per = group // STEP
    for k in order:
        span = pl.ds(k * group, group)
        if proxied:
            @pl.when(at_end)
            def _():
                p_copy(k).wait_recv()
                acc[span, :] += precv[span, :].astype(F32)
        elif n_chan > 1:
            for way in range(2):
                block, there = source(way, n_chan - 1)

                @pl.when(there)
                def _():
                    tok_copy(block, k, way, False).wait_recv()
                    for h in range(n_rep):
                        multiply(block, span, h)

        qbuf[HALO + k * group : HALO + (k + 1) * group, :] = acc[span, :].astype(BF16).astype(F32)
        if k == parts - 1:
            hsend[...] = qbuf[rows:, :].astype(BF16)

            @pl.when(s < n_seq - 1)
            def _():
                halo_copy.start()

            lax.fori_loop(k * per + 1, blocks, first, 0)
        else:
            if k == 0:
                @pl.when(s > 0)
                def _():
                    halo_copy.wait_recv()
                    qbuf[:HALO, :] = hrecv[...].astype(F32)

                @pl.when(s == 0)
                def _():
                    qbuf[:HALO, :] = jnp.zeros((HALO, 3 * ch), F32)

            lax.fori_loop(k * per, (k + 1) * per + (1 if k == parts - 2 else 0), first, 0)

    leap = jnp.exp(-rate * float(STEP))

    def scan(b, state):
        return leap * state + ubuf[b]

    ssend[...] = lax.fori_loop(0, blocks, scan, jnp.zeros((modes, ch), F32))

    def s_copy(o):
        return pltpu.make_async_remote_copy(
            src_ref=ssend,
            dst_ref=srecv.at[o],
            send_sem=ssend_sem.at[o],
            recv_sem=srecv_sem.at[o],
            device_id={"seq": lax.rem(s + o, n_seq)},
            device_id_type=MESH,
        )

    for o in range(1, n_seq):
        @pl.when(s + o < n_seq)
        def _():
            s_copy(o).start()

    acc2[:modes, :ch] = jnp.zeros((modes, ch), F32)
    for o in range(1, n_seq):
        @pl.when(s >= o)
        def _():
            s_copy(o).wait_recv()
            acc2[:modes, :ch] += jnp.exp(-rate * float(rows * (o - 1))) * srecv[o]

    def second(b, state):
        base = pl.multiple_of(b * STEP, STEP)
        total = local[pl.ds(base, STEP), :]
        for m in range(modes):
            total = total + t_out[m] * state[m : m + 1]
        longc = total.astype(BF16).astype(F32)
        gbuf[c, pl.ds(base, STEP), :] = (query[pl.ds(base, STEP), :] * longc).astype(BF16)
        return leap * state + ubuf[b]

    def g_copy(block, k, way):
        place = gbuf.at[block, pl.ds(k * group, group)]
        return pltpu.make_async_remote_copy(
            src_ref=place,
            dst_ref=place,
            send_sem=gsend_sem.at[way, block, k],
            recv_sem=grecv_sem.at[block, k],
            device_id={"chan": c + (1 if way == 0 else -1)},
            device_id_type=MESH,
        )

    state = acc2[:modes, :ch]
    for k in range(parts):
        state = lax.fori_loop(k * per, (k + 1) * per, second, state)
        for way in range(2):
            @pl.when(can_send(way))
            def _():
                g_copy(c, k, way).start()

    own_wout.wait()
    width = acc2.shape[1]
    tile = min(512, width)

    def project(block, opening):
        def one(i, carry):
            cols = pl.ds(pl.multiple_of(i * tile, tile), tile)
            part = jnp.dot(gbuf[block], woutbuf[block, :, cols], preferred_element_type=F32)
            if opening:
                acc2[:, cols] = part
            else:
                acc2[:, cols] += part
            return carry

        lax.fori_loop(0, width // tile, one, 0)

    project(c, True)
    for d in range(1, n_chan):
        for k in range(parts):
            for way in range(2):
                block, there = source(way, d)

                @pl.when(there)
                def _():
                    g_copy(block, k, way).wait_recv()

                    if d < n_chan - 1:
                        @pl.when(can_send(way))
                        def _():
                            g_copy(block, k, way).start()

        for e in range(1, n_chan - 1) if d == n_chan - 2 else [d] if d == n_chan - 1 else []:
            for way in range(2):
                block, there = source(way, e)

                @pl.when(there)
                def _():
                    project(block, False)

    out_ref[...] = acc2[...].astype(BF16)

    for d in range(n_chan - 1):
        for way in range(2):
            block, there = source(way, d)

            @pl.when(there & can_send(way))
            def _():
                for k in range(parts):
                    if d < reach:
                        tok_copy(block, k, way, d == 0).wait_send()
                    g_copy(block, k, way).wait_send()

    for o in range(1, n_seq):
        for q in range(wparts):
            (relay(q) if proxied and o == 3 else w_copy(o, q, False)).wait_send()
        for p in range(1, n_rep):
            x_copy(o, p, False).wait_send()

        @pl.when(s + o < n_seq)
        def _():
            s_copy(o).wait_send()

    if proxied:
        @pl.when(at_end)
        def _():
            for q in range(wparts):
                f_copy(q).wait_send()

        @pl.when(jnp.logical_not(at_end))
        def _():
            for q in range(wparts):
                for p in range(1, n_rep):
                    y_copy(p, q, False).wait_send()
            for k in range(parts):
                p_copy(k).wait_send()

    @pl.when(s < n_seq - 1)
    def _():
        halo_copy.wait_send()


def on_device(tokens, w_in, short_taps, decay, residue, skip, w_out):
    n_seq, n_chan, n_rep = (lax.axis_size(a) for a in ("seq", "chan", "rep"))
    rows, depth = tokens.shape
    ch, branches, wdepth = w_in.shape
    modes = decay.shape[0]
    width = w_out.shape[1]
    piece = min(512, depth, wdepth)
    parts = 4
    half = branches * ch // n_rep
    w = w_in.transpose(1, 0, 2).reshape(n_rep, half, wdepth)
    dims = (n_seq, n_chan, n_rep, parts, piece, rows, ch)
    vmem = pl.BlockSpec(memory_space=pltpu.VMEM)
    hbm = pl.BlockSpec(memory_space=pl.ANY)
    dma = pltpu.SemaphoreType.DMA
    return pl.pallas_call(
        functools.partial(kernel, dims),
        out_shape=jax.ShapeDtypeStruct((rows, width), BF16),
        in_specs=[hbm, hbm, vmem, vmem, vmem, vmem, hbm],
        out_specs=vmem,
        scratch_shapes=[
            pltpu.VMEM((n_chan, rows, depth), BF16),
            pltpu.VMEM((n_rep, n_seq, half, wdepth), BF16),
            pltpu.VMEM((n_chan, ch, width), BF16),
            pltpu.VMEM((rows, branches * ch), F32),
            pltpu.VMEM((rows + HALO, branches * ch), F32),
            pltpu.VMEM((HALO, branches * ch), BF16),
            pltpu.VMEM((HALO, branches * ch), BF16),
            pltpu.VMEM((rows, ch), F32),
            pltpu.VMEM((rows, ch), F32),
            pltpu.VMEM((rows // STEP, modes, ch), F32),
            pltpu.VMEM((modes, ch), F32),
            pltpu.VMEM((n_seq, modes, ch), F32),
            pltpu.VMEM((STEP, modes, ch), F32),
            pltpu.VMEM((modes, STEP, ch), F32),
            pltpu.VMEM((STEP, STEP, ch), F32),
            pltpu.VMEM((n_chan, rows, ch), BF16),
            pltpu.VMEM((rows, width), F32),
            pltpu.VMEM((n_rep, half, wdepth), BF16),
            pltpu.VMEM((rows, branches * ch), F32),
            pltpu.VMEM((rows, branches * ch), BF16),
            pltpu.VMEM((rows, branches * ch), BF16),
            dma((2 + n_rep,)),
            dma((2, n_chan, parts)),
            dma((n_chan, parts)),
            dma((n_seq, 4)),
            dma((n_seq, 4)),
            dma((n_seq, n_rep)),
            dma((n_seq, n_rep)),
            dma((4,)),
            dma((4,)),
            dma((n_rep, 4)),
            dma((n_rep, 4)),
            dma((parts,)),
            dma((parts,)),
            dma(()),
            dma(()),
            dma((n_seq,)),
            dma((n_seq,)),
            dma((2, n_chan, parts)),
            dma((n_chan, parts)),
        ],
        compiler_params=pltpu.CompilerParams(
            collective_id=0, has_side_effects=True, vmem_limit_bytes=56 * 1024 * 1024
        ),
        cost_estimate=pl.CostEstimate(
            flops=2 * rows * (n_chan * depth * branches * ch + n_chan * ch * width),
            bytes_accessed=2 * (rows * depth + branches * ch * wdepth + n_chan * ch * width),
            transcendentals=0,
        ),
    )(tokens, w, short_taps, decay, residue, skip.reshape(1, ch), w_out.reshape(n_chan, ch, width))


def solution(mesh):
    placed = (
        P(("rep", "seq"), "chan"),
        P("chan", None, "seq"),
        P(None, None, "chan"),
        P(None, "chan"),
        P(None, "chan"),
        P("chan"),
        P(None, "chan"),
    )
    return jax.shard_map(
        on_device, mesh=mesh, in_specs=placed, out_specs=P(("rep", "seq"), "chan"), check_vma=False
    )
```
